128 devices in a mesh: ctx: 32 (over z, x_hi, y), head: 4 (over x_lo, core).
Axes of the slice: x: 4 (x_hi: 2, x_lo: 2; x = x_hi * 2 + x_lo), y: 4, z: 4, core: 2. Of those that a mesh axis runs over, the one named last changes fastest.
Arguments:
- query: bfloat16 [4096, 36864], P('ctx', 'head'), may hold values from -16 to 16
- compressed: bfloat16 [4096, 576], P('ctx'), may hold values from -8 to 8
- segments: int32 [4096], replicated, may hold values from 0 to 2, never falling along the last dimension, each value on 1 to 3072 neighbouring positions
- grad_attn: bfloat16 [4096, 32768], P('ctx', 'head'), may hold values from -6 to 6
Outputs:
- attention: float32 [4096, 32768], P('ctx', 'head')
- grad_query: float32 [4096, 36864], P('ctx', 'head')
- grad_compressed: float32 [4096, 576], P('ctx', 'head')
The draws below stay inside these ranges and needn't reach their ends.
Inputs may be any that keep to these rules, and one draw needn't show every extreme that they name: `segments`: segment numbers never fall along the trajectory.
All inputs are finite; a program needn't handle non-finite values.
Results may differ from the reference program's by a relative error of at most 0.018.
Values may be sent and summed in bfloat16 or wider, within the bound.
No kernel may reach another device: no remote copies, remote signals or barrier semaphores. Data moves between devices by JAX's collectives and lax.ppermute only.
A program may use at most 128 MiB of HBM per device.

```python
import math
import jax
import jax.numpy as jnp
import numpy as np
from jax import lax

LATENT = 512
ROPE = 64
HEADS = 64
SEQ = 4096


def shared_keys(key, align_weight):
    feature_width = LATENT + ROPE
    drawn = jax.random.truncated_normal(key, -4.0, 4.0, (SEQ, feature_width), jnp.float32)
    chosen = jax.random.bernoulli(jax.random.fold_in(key, 11), 1.0 / 32, (SEQ,))
    positions = jnp.arange(SEQ)
    chosen = chosen & (positions % 2 == 0) & (positions > 0)
    levels = jnp.array([4.0, 8.0, 12.0], jnp.float32)
    strength = levels[jax.random.randint(jax.random.fold_in(key, 12), (SEQ,), 0, 3)]
    jitter = jax.random.truncated_normal(jax.random.fold_in(key, 13), -4.0, 4.0, (SEQ, ROPE), jnp.float32)
    rotary = drawn[:, LATENT:]
    signs = jnp.where(rotary >= 0.0, 1.0, -1.0)
    strong = 7.0 * signs
    next_strong = jnp.roll(strong, -1, axis=0)
    next_chosen = jnp.roll(chosen, -1)
    next_strength = jnp.roll(strength, -1)
    partner = jnp.clip(next_strong + jitter * (3.5 / (0.576 * next_strength))[:, None], -8.0, 8.0)
    use_own = (chosen & (align_weight > 0))[:, None]
    use_partner = (next_chosen & (align_weight > 0))[:, None]
    rotary = jnp.where(use_own, strong, jnp.where(use_partner, partner, rotary))
    return (drawn[:, :LATENT], rotary)


def draw_compressed(key, part):
    latent, rotary = shared_keys(key, 0.0)
    return jnp.concatenate([latent, rotary], axis=1).astype(jnp.bfloat16)


def draw_query(key, part):
    feature_width = LATENT + ROPE
    key = jax.random.fold_in(key, 5)
    drawn = 0.5 * jax.random.truncated_normal(key, -4.0, 4.0, (SEQ, HEADS, feature_width), jnp.float32)
    return drawn.reshape(SEQ, HEADS * feature_width).astype(jnp.bfloat16)


def steps_of(stream_key, extent, cuts, smallest, largest):
    level, own = 1.0, jax.random.fold_in(stream_key, 6)
    for dim, shards_of in cuts:
        heights = jnp.exp(jax.random.uniform(jax.random.fold_in(own, dim), (shards_of,), jnp.float32, smallest / len(cuts), largest / len(cuts)))
        level = level * jnp.repeat(heights, extent[dim] // shards_of).reshape([-1 if axis == dim else 1 for axis in range(len(extent))])
    return level


def profile(amount, total, most, skew):
    loads = [(1 << 20) // math.isqrt(standing ** skew) + 1 for standing in range(2, amount + 1)]
    surplus, given = total - most - (amount - 1), [1] * (amount - 1)
    while surplus > 0:
        movable = [i for i in range(amount - 1) if given[i] < most]
        pool, left = sum([loads[i] for i in movable]), surplus
        for i in movable:
            extra = min(most - given[i], max(1, left * loads[i] // pool), surplus)
            given[i] = given[i] + extra
            surplus = surplus - extra
    return np.array([most] + given)


def ragged(own_key, amount, total, limit, skew):
    if amount == 2:
        one = jax.random.randint(own_key, (), max(1, total - limit), min(limit, total - 1) + 1)
        return jnp.stack([one, total - one])
    sizes = jnp.asarray(profile(amount, total, limit, skew), jnp.int32)
    pairs = (amount - 1) // 2
    donor, taker = sizes[1:1 + 2 * pairs:2], sizes[2:2 + 2 * pairs:2]
    room = jnp.minimum(donor - 1, limit - taker)
    passed = jax.random.randint(jax.random.fold_in(own_key, 1), (pairs,), 0, 1 << 20) % (room + 1)
    sizes = sizes.at[1:1 + 2 * pairs:2].set(donor - passed).at[2:2 + 2 * pairs:2].set(taker + passed)
    return sizes[jax.random.permutation(jax.random.fold_in(own_key, 2), amount)]


def scatter_about(key, dims, spread, bound, split=(), kind=jnp.bfloat16):
    entries = spread * jax.random.normal(key, dims, jnp.float32)
    if split:
        entries = entries * steps_of(key, dims, split, -0.22, 0.18)
    return jnp.clip(entries, -bound, bound).astype(kind)


def setup_inputs(seed: int = 0) -> dict:
    arg_keys = jax.random.split(jax.random.key(seed), 5)
    query = draw_query(jax.random.fold_in(arg_keys[4], 71), 0)
    compressed = draw_compressed(jax.random.fold_in(arg_keys[4], 71), 0)
    segments = jnp.searchsorted(jnp.cumsum(ragged(arg_keys[2], 3, SEQ, 3 * SEQ // 4, 0)), jnp.arange(SEQ), side="right").astype(jnp.int32)
    grad_attn = scatter_about(arg_keys[3], (SEQ, HEADS * LATENT), 1.0, 6.0, ((0, 32), (1, 4)))
    return dict(query=query, compressed=compressed, segments=segments, grad_attn=grad_attn)


score_scale = 1.0 / math.sqrt(192.0)

def reference(query, compressed, segments, grad_attn):
    feature_width = LATENT + ROPE
    row_count = math.gcd(SEQ, 128)
    blocks = SEQ // row_count
    query_blocks = query.reshape(blocks, row_count, HEADS, feature_width)
    grad_blocks = grad_attn.reshape(blocks, row_count, HEADS, LATENT)
    keys_wide = compressed.astype(jnp.float32)
    values_wide = keys_wide[:, :LATENT]
    positions = jnp.arange(SEQ, dtype=jnp.int32)

    def one_block(running, inputs):
        query_block, grad_block, block_index = inputs
        query_wide = query_block.astype(jnp.float32)
        grad_wide = grad_block.astype(jnp.float32)
        first_row = (block_index * row_count).astype(jnp.int32)
        query_position = first_row + jnp.arange(row_count, dtype=jnp.int32)
        query_segment = lax.dynamic_slice_in_dim(segments, first_row, row_count)
        visible = (positions[None, :] <= query_position[:, None]) & (segments[None, :] == query_segment[:, None])
        visible = visible[:, None, :]
        scores = jnp.einsum('thc,kc->thk', query_wide, keys_wide) * score_scale
        masked = jnp.where(visible, scores, -jnp.inf)
        row_max = lax.optimization_barrier(jnp.max(masked, axis=-1))
        log_total = row_max + jnp.log(lax.optimization_barrier(jnp.sum(jnp.exp(masked - row_max[..., None]), axis=-1)))
        probabilities = jnp.where(visible, jnp.exp(scores - log_total[..., None]), jnp.float32(0.0))
        softmax_weights = probabilities.astype(jnp.bfloat16)
        attended = jnp.einsum('thk,kc->thc', softmax_weights.astype(jnp.float32), values_wide)
        row_dots = lax.optimization_barrier(jnp.sum(grad_wide * attended, axis=-1))
        weight_grads = jnp.einsum('thc,kc->thk', grad_wide, values_wide)
        score_grads = (probabilities * (weight_grads - row_dots[..., None]) * score_scale).astype(jnp.bfloat16)
        score_wide = score_grads.astype(jnp.float32)
        query_grad = jnp.einsum('thk,kc->thc', score_wide, keys_wide)
        key_grad = jnp.einsum('thk,thc->kc', score_wide, query_wide)
        value_grad = jnp.einsum('thk,thc->kc', softmax_weights.astype(jnp.float32), grad_wide)
        value_grad = jnp.concatenate([value_grad, jnp.zeros((SEQ, ROPE), jnp.float32)], axis=1)
        return (running + key_grad + value_grad, (attended, query_grad))
    starting = jnp.zeros((SEQ, feature_width), jnp.float32)
    indices = jnp.arange(blocks, dtype=jnp.int32)
    key_grads, (attended, query_grad) = lax.scan(one_block, starting, (query_blocks, grad_blocks, indices))
    return (attended.reshape(SEQ, HEADS * LATENT), query_grad.reshape(SEQ, HEADS * feature_width), key_grads)
```

```python
import math

import jax
import jax.numpy as jnp
from jax import lax
from jax.experimental import pallas as pl
from jax.experimental.pallas import tpu as pltpu
from jax.sharding import PartitionSpec as P

LATENT = 512
ROPE = 64
WIDTH = LATENT + ROPE
ROWS = 128
GROUPS = 16
LANES = ROWS * GROUPS
SEQ = 4096
HALF = WIDTH // 2
PART = WIDTH // 4
KB = 512
MAXB = 7
HEADS = 4
CHUNK = HEADS * ROWS
STEPS = LANES // CHUNK

SCALE = 1.0 / math.sqrt(192.0)
SCALE2 = SCALE * math.log2(math.e)
NEG = -1e30

NZ, NXH, NY, NXL, NC = 4, 2, 4, 2, 2
F32, BF16 = jnp.float32, jnp.bfloat16


def flat(z, xh, y, xl, c):
    return ((z * NXH + xh) * NY + y) * (NXL * NC) + xl * NC + c


def send(x, move):
    pairs = []
    for z in range(NZ):
        for xh in range(NXH):
            for y in range(NY):
                for xl in range(NXL):
                    for c in range(NC):
                        to = move(z, xh, y, xl, c)
                        pairs.append((flat(z, xh, y, xl, c), flat(*to)))
    return lax.ppermute(x, ("ctx", "head"), pairs)


def other_core(z, xh, y, xl, c):
    return (z, xh, y, xl, 1 - c)


def across_x(z, xh, y, xl, c):
    return (z, 1 - xh, y, 1 - xl, c)


def along_x(dxh, dxl):
    return lambda z, xh, y, xl, c: (z, (xh + dxh) % NXH, y, (xl + dxl) % NXL, c)


def along(axis, d):
    def move(z, xh, y, xl, c):
        if c == axis:
            return ((z + d) % NZ, xh, y, xl, c)
        return (z, xh, (y + d) % NY, xl, c)

    return move


def collect(own, core):
    mine = lax.dynamic_slice_in_dim(own.T, core * HALF, HALF, 0)
    pair = jnp.stack([mine, send(mine, across_x)])
    near = jnp.stack([pair] + [send(pair, along(1, d)) for d in (1, 3, 2)])
    below, above = send(near, along(0, 1)), send(near, along(0, 3))
    pieces = [near, below, above, send(below, along(0, 1))]
    return pieces + [send(p, other_core) for p in pieces]


RING = (0, -1, 1, 2)


def attend_kernel(segments, q_ref, qnext_ref, g_ref, *rest):
    pieces = rest[:8]
    o_ref, dq_ref, keep_ref, send_ref = rest[8:12]
    (c_v, ct_v, s_v, w_v, acc, qt, gt, qn, gn, top_v, oacc, dqacc, st_f, st_b, zero_f, zero_b,
     in_sem, out_sem, zero_sem) = rest[12:]
    step = pl.program_id(0)
    ctx, head = lax.axis_index("ctx"), lax.axis_index("head")
    z, xh, y, xl, core = ctx >> 3, (ctx >> 2) & 1, ctx & 3, head >> 1, head & 1

    def bound(value):
        def halve(_, ends):
            low, high = ends
            mid = (low + high) >> 1
            less = (low < high) & (segments[jnp.minimum(mid, SEQ - 1)] < value)
            return jnp.where(less, mid + 1, low), jnp.where(less, high, mid)

        return lax.fori_loop(0, 13, halve, (jnp.int32(0), jnp.int32(SEQ)))[0]

    second, third = bound(1), bound(2)

    def start_of(position):
        return jnp.where(position >= third, third, jnp.where(position >= second, second, 0))

    first_row = ctx * ROWS
    first = start_of(first_row) // KB
    blocks = (first_row + ROWS + KB - 1) // KB - first
    free_low, free_high = start_of(first_row + ROWS - 1), first_row + 1
    token = first_row + (lax.broadcasted_iota(jnp.int32, (1, CHUNK), 1) & (ROWS - 1))
    start = start_of(token)

    def off(kb):
        return pl.multiple_of((first + kb) * KB, KB)

    def blk(kb):
        return pl.multiple_of(kb * KB, KB)

    def live(block):
        return (block >= first) & (block < first + blocks)

    def fetch(piece, to, half):
        return pltpu.make_async_copy(
            piece,
            ct_v.at[
                pl.ds(pl.multiple_of(half * HALF, 32), HALF),
                pl.ds(pl.multiple_of(to * ROWS, ROWS), ROWS),
            ],
            in_sem.at[to, half],
        )

    def fetch_all():
        for n in range(64):
            other, piece, slot, x = n // 32, n // 8 % 4, n // 2 % 4, n % 2
            half = 1 - core if other else core
            dy = jnp.where(half == 0, RING[slot], RING[piece])
            dz = jnp.where(half == 0, RING[piece], RING[slot])
            to = ((z + dz) & 3) * 8 + (xh ^ x) * 4 + ((y + dy) & 3)

            @pl.when(live(to >> 2))
            def _():
                fetch(pieces[other * 4 + piece].at[slot, x], to, half).start()

    def placed(ref, own, block):
        dz, x = ((block >> 1) - z) & 3, (block & 1) ^ xh
        return ref.at[dz, :, x] if own == 0 else ref.at[:, dz, x]

    def by_core(act):
        for c in range(NC):
            @pl.when(core == c)
            def _():
                act(c)

    def clear(block, act):
        def copies(c):
            act(pltpu.make_async_copy(zero_f, placed(keep_ref, c, block), zero_sem.at[0, block]))
            act(pltpu.make_async_copy(zero_b, placed(send_ref, 1 - c, block), zero_sem.at[1, block]))

        @pl.when(jnp.logical_not(live(block)))
        def _():
            by_core(copies)

    def deliver_block(kb, act):
        slot = lax.rem(kb, 2)

        def copies(c):
            act(pltpu.make_async_copy(
                st_f.at[slot, :, :, c], placed(keep_ref, c, first + kb), out_sem.at[0, slot]
            ))
            act(pltpu.make_async_copy(
                st_b.at[slot, :, :, 1 - c], placed(send_ref, 1 - c, first + kb), out_sem.at[1, slot]
            ))

        by_core(copies)

    def begin(copy):
        copy.start()

    def end(copy):
        copy.wait()

    def turn_query(ref):
        turned = ref[...].T
        for h in range(HEADS):
            qt[:, h * ROWS:(h + 1) * ROWS] = turned[h * WIDTH:(h + 1) * WIDTH]

    def score(kb, n, masked):
        rows = n * KB
        s = jnp.dot(c_v[pl.ds(off(kb), rows), :], qt[...], preferred_element_type=F32)
        if masked:
            key = off(kb) + lax.broadcasted_iota(jnp.int32, (rows, CHUNK), 0)
            s = jnp.where((key >= start) & (key <= token), s, NEG)
        return s

    def keep_score(kb, n, s, top):
        rows = n * KB
        s_v[pl.ds(blk(kb), rows), :] = s
        return jnp.maximum(top, jnp.max(s.reshape(rows // 8, 8, CHUNK), axis=0))

    def sweep(body, carried):
        pairs = blocks // 2
        carried = lax.fori_loop(0, pairs, lambda i, c: body(2 * i, 2, c), carried)
        return lax.fori_loop(2 * pairs, blocks, lambda i, c: body(i, 1, c), carried)

    lowest = jnp.full((8, CHUNK), NEG, F32)

    @pl.when(step == 0)
    def _():
        fetch_all()
        zero_f[...] = jnp.zeros_like(zero_f)
        zero_b[...] = jnp.zeros_like(zero_b)
        for block in range(SEQ // KB):
            clear(block, begin)
        turn_query(q_ref)

        def turn(kb, top):
            for t in range(KB // ROWS):
                for half in range(2):
                    fetch(pieces[0].at[0, 0], (first + kb) * (KB // ROWS) + t, half).wait()
            c_v[pl.ds(off(kb), KB), :] = ct_v[:, pl.ds(off(kb), KB)].T
            acc[pl.ds(blk(kb), KB), :] = jnp.zeros((KB, WIDTH), F32)
            return keep_score(kb, 1, score(kb, 1, True), top)

        top_v[...] = lax.fori_loop(0, blocks, turn, lowest)

    turned = g_ref[...].T
    for h in range(HEADS):
        lanes = slice(h * ROWS, (h + 1) * ROWS)
        gt[:, lanes] = turned[h * LATENT:(h + 1) * LATENT]
        gn[lanes, :] = g_ref[:, h * LATENT:(h + 1) * LATENT]
        qn[lanes, :] = q_ref[:, h * WIDTH:(h + 1) * WIDTH]
    turn_query(qnext_ref)

    top = jnp.max(top_v[...], axis=0, keepdims=True)
    oacc[...] = jnp.zeros_like(oacc)

    def values(kb, n, total):
        b, rows = blk(kb), n * KB
        w_v[pl.ds(b, rows), :] = jnp.dot(
            c_v[pl.ds(off(kb), rows), :LATENT], gt[...], preferred_element_type=F32
        )
        e = jnp.exp2((s_v[pl.ds(b, rows), :] - top) * SCALE2)
        s_v[pl.ds(b, rows), :] = e
        oacc[...] += jnp.dot(
            ct_v[:LATENT, pl.ds(off(kb), rows)], e.astype(BF16), preferred_element_type=F32
        )
        return total + jnp.sum(e.reshape(rows // 8, 8, CHUNK), axis=0)

    total = sweep(values, jnp.zeros((8, CHUNK), F32))
    inverse = 1.0 / jnp.sum(total, axis=0, keepdims=True)
    out = oacc[...] * inverse
    dots = jnp.sum(gt[...].astype(F32) * out, axis=0, keepdims=True)
    for h in range(HEADS):
        o_ref[:, h * LATENT:(h + 1) * LATENT] = out[:, h * ROWS:(h + 1) * ROWS].T

    dqacc[...] = jnp.zeros_like(dqacc)

    def grads(kb, n):
        b, rows = blk(kb), n * KB
        p = s_v[pl.ds(b, rows), :] * inverse
        ds = (p * (w_v[pl.ds(b, rows), :] - dots) * SCALE).astype(BF16)
        p = p.astype(BF16)
        dqacc[...] += jnp.dot(ct_v[:, pl.ds(off(kb), rows)], ds, preferred_element_type=F32)
        dk = acc[pl.ds(b, rows), :] + jnp.dot(ds, qn[...], preferred_element_type=F32)
        dv = jnp.dot(p, gn[...], preferred_element_type=F32)
        return jnp.concatenate([dk[:, :LATENT] + dv, dk[:, LATENT:]], axis=1)

    @pl.when(step < STEPS - 1)
    def _():
        def both(kb, n, top):
            def body(masked):
                def run(top):
                    s = score(kb, n, masked)
                    acc[pl.ds(blk(kb), n * KB), :] = grads(kb, n)
                    return keep_score(kb, n, s, top)

                return run

            free = (off(kb) >= free_low) & (off(kb) + n * KB <= free_high)
            return lax.cond(free, body(False), body(True), top)

        top_v[...] = sweep(both, lowest)

    @pl.when(step == STEPS - 1)
    def _():
        def last(kb, _):
            turned = grads(kb, 1).T

            @pl.when(kb >= 2)
            def _():
                deliver_block(kb - 2, end)

            slot = lax.rem(kb, 2)
            for t in range(NY):
                tile = turned[:, t * ROWS:(t + 1) * ROWS].reshape(NXL, NC, PART, ROWS)
                for side in range(NXL):
                    st_f[slot, (t - y) & 3, side ^ xl] = tile[side]
                    st_b[slot, (t - y) & 3, side ^ xl] = tile[side].astype(BF16)
            deliver_block(kb, begin)
            return 0

        lax.fori_loop(0, blocks, last, 0)

    dq = dqacc[...]
    dq_ref[...] = jnp.concatenate(
        [dq[:, h * ROWS:(h + 1) * ROWS] for h in range(HEADS)], axis=0
    ).T

    @pl.when(step == STEPS - 1)
    def _():
        def finish(kb, _):
            deliver_block(kb, end)
            return 0

        lax.fori_loop(jnp.maximum(blocks - 2, 0), blocks, finish, 0)
        for block in range(SEQ // KB):
            clear(block, end)


def attend(segments, query, grad, pieces):
    any_spec = pl.BlockSpec(memory_space=pl.ANY)
    tile = (NY, NXL, PART, ROWS)
    staged = (2, NY, NXL, NC, PART, ROWS)
    rings = (NZ, NY, NXH, NXL, PART, ROWS)
    return pl.pallas_call(
        attend_kernel,
        grid_spec=pltpu.PrefetchScalarGridSpec(
            num_scalar_prefetch=1,
            grid=(STEPS,),
            in_specs=[
                pl.BlockSpec((ROWS, HEADS * WIDTH), lambda i, s: (0, i)),
                pl.BlockSpec(
                    (ROWS, HEADS * WIDTH), lambda i, s: (0, jnp.minimum(i + 1, STEPS - 1))
                ),
                pl.BlockSpec((ROWS, HEADS * LATENT), lambda i, s: (0, i)),
            ] + [any_spec] * 8,
            out_specs=[
                pl.BlockSpec((ROWS, HEADS * LATENT), lambda i, s: (0, i)),
                pl.BlockSpec((ROWS, HEADS * WIDTH), lambda i, s: (0, i)),
                any_spec,
                any_spec,
            ],
            scratch_shapes=[
                pltpu.VMEM((SEQ, WIDTH), BF16),
                pltpu.VMEM((WIDTH, SEQ), BF16),
                pltpu.VMEM((MAXB * KB, CHUNK), F32),
                pltpu.VMEM((MAXB * KB, CHUNK), F32),
                pltpu.VMEM((MAXB * KB, WIDTH), F32),
                pltpu.VMEM((WIDTH, CHUNK), BF16),
                pltpu.VMEM((LATENT, CHUNK), BF16),
                pltpu.VMEM((CHUNK, WIDTH), BF16),
                pltpu.VMEM((CHUNK, LATENT), BF16),
                pltpu.VMEM((8, CHUNK), F32),
                pltpu.VMEM((LATENT, CHUNK), F32),
                pltpu.VMEM((WIDTH, CHUNK), F32),
                pltpu.VMEM(staged, F32),
                pltpu.VMEM(staged, BF16),
                pltpu.VMEM(tile, F32),
                pltpu.VMEM(tile, BF16),
                pltpu.SemaphoreType.DMA((SEQ // ROWS, 2)),
                pltpu.SemaphoreType.DMA((2, 2)),
                pltpu.SemaphoreType.DMA((2, SEQ // KB)),
            ],
        ),
        out_shape=[
            jax.ShapeDtypeStruct((ROWS, GROUPS * LATENT), F32),
            jax.ShapeDtypeStruct((ROWS, GROUPS * WIDTH), F32),
            jax.ShapeDtypeStruct(rings, F32),
            jax.ShapeDtypeStruct(rings, BF16),
        ],
        compiler_params=pltpu.CompilerParams(
            dimension_semantics=("arbitrary",), vmem_limit_bytes=58 * 1024 * 1024
        ),
        cost_estimate=pl.CostEstimate(
            flops=40 * 10**9, bytes_accessed=30 * 10**6, transcendentals=10**7
        ),
        name="attend",
    )(segments, query, query, grad, *pieces)


def deliver(keep, out):
    got = send(out, other_core)

    def part(i):
        return keep[i] + got[i].astype(F32)

    def wide(x):
        return x.astype(F32)

    far = send(part(2).astype(BF16), along(0, 1))
    down = send(part(3).astype(BF16), along(0, 3))
    up = send((part(1) + wide(far)).astype(BF16), along(0, 1))
    total = part(0) + wide(up) + wide(down)
    parts = total.astype(BF16)
    ring = [wide(send(parts[d], along(1, d))) for d in (1, 3, 2)]
    total = total[0] + ring[0] + ring[1] + ring[2]
    parts = total.astype(BF16)
    ring = [wide(send(parts[a, b], along_x(a, b))) for a, b in ((0, 1), (1, 1), (1, 0))]
    return total[0, 0] + ring[0] + ring[1] + ring[2]


def shards(query, compressed, segments, grad_attn):
    pieces = collect(compressed, lax.axis_index("head") % NC)
    attended, query_grad, keep, out = attend(segments, query, grad_attn, pieces)
    return attended, query_grad, deliver(keep, out).T


def solution(mesh):
    placed = (P("ctx", "head"), P("ctx", None), P(), P("ctx", "head"))
    return jax.shard_map(
        shards,
        mesh=mesh,
        in_specs=placed,
        out_specs=(P("ctx", "head"), P("ctx", "head"), P("ctx", "head")),
        check_vma=False,
    )
```

```python
import math

import jax
import jax.numpy as jnp
from jax import lax
from jax.experimental import pallas as pl
from jax.experimental.pallas import tpu as pltpu
from jax.sharding import PartitionSpec as P

LATENT = 512
ROPE = 64
WIDTH = LATENT + ROPE
ROWS = 128
GROUPS = 16
LANES = ROWS * GROUPS
SEQ = 4096
HALF = WIDTH // 2
PART = WIDTH // 4
KB = 512
MAXB = 7
HEADS = 4
CHUNK = HEADS * ROWS
STEPS = LANES // CHUNK

SCALE = 1.0 / math.sqrt(192.0)
SCALE2 = SCALE * math.log2(math.e)
NEG = -1e30

NZ, NXH, NY, NXL, NC = 4, 2, 4, 2, 2
F32, BF16 = jnp.float32, jnp.bfloat16


def flat(z, xh, y, xl, c):
    return ((z * NXH + xh) * NY + y) * (NXL * NC) + xl * NC + c


def send(x, move):
    pairs = []
    for z in range(NZ):
        for xh in range(NXH):
            for y in range(NY):
                for xl in range(NXL):
                    for c in range(NC):
                        to = move(z, xh, y, xl, c)
                        pairs.append((flat(z, xh, y, xl, c), flat(*to)))
    return lax.ppermute(x, ("ctx", "head"), pairs)


def other_core(z, xh, y, xl, c):
    return (z, xh, y, xl, 1 - c)


def across_x(z, xh, y, xl, c):
    return (z, 1 - xh, y, 1 - xl, c)


def along_x(dxh, dxl):
    return lambda z, xh, y, xl, c: (z, (xh + dxh) % NXH, y, (xl + dxl) % NXL, c)


def along(axis, d):
    def move(z, xh, y, xl, c):
        if c == axis:
            return ((z + d) % NZ, xh, y, xl, c)
        return (z, xh, (y + d) % NY, xl, c)

    return move


def collect(own, core):
    mine = lax.dynamic_slice_in_dim(own.T, core * HALF, HALF, 0)
    pair = jnp.stack([mine, send(mine, across_x)])
    near = jnp.stack([pair] + [send(pair, along(1, d)) for d in (1, 3, 2)])
    below, above = send(near, along(0, 1)), send(near, along(0, 3))
    pieces = [near, below, above, send(below, along(0, 1))]
    return pieces + [send(p, other_core) for p in pieces]


RING = (0, -1, 1, 2)


def attend_kernel(segments, q_ref, g_ref, *rest):
    pieces = rest[:8]
    o_ref, dq_ref, keep_ref, send_ref = rest[8:12]
    (c_v, ct_v, s_v, e_v, acc, qt, gt, qn, gn, top_v, total_v, oacc, dqacc, dq_st, st_f, st_b,
     zero_f, zero_b, in_sem, out_sem, zero_sem, dq_sem) = rest[12:]
    step = pl.program_id(0)
    ctx, head = lax.axis_index("ctx"), lax.axis_index("head")
    z, xh, y, xl, core = ctx >> 3, (ctx >> 2) & 1, ctx & 3, head >> 1, head & 1

    def bound(value):
        def halve(_, ends):
            low, high = ends
            mid = (low + high) >> 1
            less = (low < high) & (segments[jnp.minimum(mid, SEQ - 1)] < value)
            return jnp.where(less, mid + 1, low), jnp.where(less, high, mid)

        return lax.fori_loop(0, 13, halve, (jnp.int32(0), jnp.int32(SEQ)))[0]

    second, third = bound(1), bound(2)

    def start_of(position):
        return jnp.where(position >= third, third, jnp.where(position >= second, second, 0))

    first_row = ctx * ROWS
    first = start_of(first_row) // KB
    blocks = (first_row + ROWS + KB - 1) // KB - first
    free_low, free_high = start_of(first_row + ROWS - 1), first_row + 1
    token = first_row + (lax.broadcasted_iota(jnp.int32, (1, CHUNK), 1) & (ROWS - 1))
    start = start_of(token)

    def off(kb):
        return pl.multiple_of((first + kb) * KB, KB)

    def blk(kb):
        return pl.multiple_of(kb * KB, KB)

    def live(block):
        return (block >= first) & (block < first + blocks)

    def fetch(piece, to, half):
        return pltpu.make_async_copy(
            piece,
            ct_v.at[
                pl.ds(pl.multiple_of(half * HALF, 32), HALF),
                pl.ds(pl.multiple_of(to * ROWS, ROWS), ROWS),
            ],
            in_sem.at[to, half],
        )

    def fetch_all():
        for n in range(64):
            other, piece, slot, x = n // 32, n // 8 % 4, n // 2 % 4, n % 2
            half = 1 - core if other else core
            dy = jnp.where(half == 0, RING[slot], RING[piece])
            dz = jnp.where(half == 0, RING[piece], RING[slot])
            to = ((z + dz) & 3) * 8 + (xh ^ x) * 4 + ((y + dy) & 3)

            @pl.when(live(to >> 2))
            def _():
                fetch(pieces[other * 4 + piece].at[slot, x], to, half).start()

    def placed(ref, own, block):
        dz, x = ((block >> 1) - z) & 3, (block & 1) ^ xh
        return ref.at[dz, :, x] if own == 0 else ref.at[:, dz, x]

    def by_core(act):
        for c in range(NC):
            @pl.when(core == c)
            def _():
                act(c)

    def clear(block, act):
        def copies(c):
            act(pltpu.make_async_copy(zero_f, placed(keep_ref, c, block), zero_sem.at[0, block]))
            act(pltpu.make_async_copy(zero_b, placed(send_ref, 1 - c, block), zero_sem.at[1, block]))

        @pl.when(jnp.logical_not(live(block)))
        def _():
            by_core(copies)

    def deliver_block(kb, act):
        slot = lax.rem(kb, 2)

        def copies(c):
            act(pltpu.make_async_copy(
                st_f.at[slot, :, :, c], placed(keep_ref, c, first + kb), out_sem.at[0, slot]
            ))
            act(pltpu.make_async_copy(
                st_b.at[slot, :, :, 1 - c], placed(send_ref, 1 - c, first + kb), out_sem.at[1, slot]
            ))

        by_core(copies)

    def begin(copy):
        copy.start()

    def end(copy):
        copy.wait()

    def heads_of(ref, width, chunk):
        lanes = pl.multiple_of(chunk * HEADS * width, 128)
        return ref[:, pl.ds(lanes, HEADS * width)]

    def turn_query(chunk):
        turned = heads_of(q_ref, WIDTH, chunk).T
        for h in range(HEADS):
            qt[:, h * ROWS:(h + 1) * ROWS] = turned[h * WIDTH:(h + 1) * WIDTH]

    def turn_grad(chunk):
        turned = heads_of(g_ref, LATENT, chunk).T
        for h in range(HEADS):
            gt[:, h * ROWS:(h + 1) * ROWS] = turned[h * LATENT:(h + 1) * LATENT]

    def take_rows(chunk):
        q = heads_of(q_ref, WIDTH, chunk)
        g = heads_of(g_ref, LATENT, chunk)
        for h in range(HEADS):
            gn[h * ROWS:(h + 1) * ROWS, :] = g[:, h * LATENT:(h + 1) * LATENT]
            qn[h * ROWS:(h + 1) * ROWS, :] = q[:, h * WIDTH:(h + 1) * WIDTH]

    def score(kb, masked):
        s = jnp.dot(c_v[pl.ds(off(kb), KB), :], qt[...], preferred_element_type=F32)
        if masked:
            key = off(kb) + lax.broadcasted_iota(jnp.int32, (KB, CHUNK), 0)
            s = jnp.where((key >= start) & (key <= token), s, NEG)
        return s

    def folded(x):
        return x.reshape(KB // 8, 8, CHUNK)

    def keep_score(kb, s, top):
        s_v[pl.ds(blk(kb), KB), :] = s
        return jnp.maximum(top, jnp.max(folded(s), axis=0))

    def turn_dq(chunk):
        dq = dqacc[...]
        dq_st[lax.rem(chunk, 2)] = jnp.concatenate(
            [dq[:, h * ROWS:(h + 1) * ROWS] for h in range(HEADS)], axis=0
        ).T

    def send_dq(chunk):
        slot = lax.rem(chunk, 2)
        lanes = pl.multiple_of(chunk * HEADS * WIDTH, 128)
        return pltpu.make_async_copy(
            dq_st.at[slot], dq_ref.at[:, pl.ds(lanes, HEADS * WIDTH)], dq_sem.at[slot]
        )

    lowest = jnp.full((8, CHUNK), NEG, F32)

    @pl.when(step == 0)
    def _():
        fetch_all()
        zero_f[...] = jnp.zeros_like(zero_f)
        zero_b[...] = jnp.zeros_like(zero_b)
        for block in range(SEQ // KB):
            clear(block, begin)
        turn_query(0)

        def turn(kb, top):
            for t in range(KB // ROWS):
                for half in range(2):
                    fetch(pieces[0].at[0, 0], (first + kb) * (KB // ROWS) + t, half).wait()
            c_v[pl.ds(off(kb), KB), :] = ct_v[:, pl.ds(off(kb), KB)].T
            acc[pl.ds(blk(kb), KB), :] = jnp.zeros((KB, WIDTH), F32)
            return keep_score(kb, score(kb, True), top)

        top_v[...] = lax.fori_loop(0, blocks, turn, lowest)
        turn_query(1)

    top = jnp.max(top_v[...], axis=0, keepdims=True)

    def exps(kb):
        e = jnp.exp2((s_v[pl.ds(blk(kb), KB), :] - top) * SCALE2)
        return e, e.astype(BF16)

    def value(kb, e):
        e_v[pl.ds(blk(kb), KB), :] = e
        return jnp.dot(ct_v[:LATENT, pl.ds(off(kb), KB)], e, preferred_element_type=F32)

    def prepare():
        turn_grad(step)
        take_rows(step)
        turn_dq(step + 1)

    @pl.when((step >= 3))
    def _():
        send_dq(step - 3).wait()

    @pl.when(step < STEPS - 1)
    def _():
        s = score(0, True)
        wide, e = exps(0)
        oacc[...] = value(0, e)
        prepare()
        carried = folded(wide).sum(axis=0), keep_score(0, s, lowest)

        def values(kb, carried):
            def body(masked):
                def run(carried):
                    total, above = carried
                    s = score(kb, masked)
                    wide, e = exps(kb)
                    oacc[...] += value(kb, e)
                    return total + folded(wide).sum(axis=0), keep_score(kb, s, above)

                return run

            free = (off(kb) >= free_low) & (off(kb) + KB <= free_high)
            return lax.cond(free, body(False), body(True), carried)

        total_v[...], top_v[...] = lax.fori_loop(1, blocks, values, carried)

    @pl.when(step == STEPS - 1)
    def _():
        wide, e = exps(0)
        oacc[...] = value(0, e)
        prepare()

        def values(kb, total):
            wide, e = exps(kb)
            oacc[...] += value(kb, e)
            return total + folded(wide).sum(axis=0)

        total_v[...] = lax.fori_loop(1, blocks, values, folded(wide).sum(axis=0))

    @pl.when(step >= 1)
    def _():
        send_dq(step - 1).start()

    inverse = 1.0 / jnp.sum(total_v[...], axis=0, keepdims=True)
    out = oacc[...] * inverse
    oacc[...] = out
    dots = jnp.sum(gt[...].astype(F32) * out, axis=0, keepdims=True)

    def grads(kb):
        w = jnp.dot(
            c_v[pl.ds(off(kb), KB), :LATENT], gt[...], preferred_element_type=F32
        )
        p = e_v[pl.ds(blk(kb), KB), :].astype(F32) * inverse
        dv = jnp.dot(p.astype(BF16), gn[...], preferred_element_type=F32)
        ds = (p * (w - dots) * SCALE).astype(BF16)
        dq = jnp.dot(ct_v[:, pl.ds(off(kb), KB)], ds, preferred_element_type=F32)
        dk = jnp.dot(ds, qn[...], preferred_element_type=F32)
        so_far = pl.ds(blk(kb), KB)
        acc[so_far, :LATENT] += dk[:, :LATENT] + dv
        acc[so_far, LATENT:] += dk[:, LATENT:]
        return dq

    dqacc[...] = grads(0)
    for h in range(HEADS):
        o_ref[:, h * LATENT:(h + 1) * LATENT] = oacc[:, h * ROWS:(h + 1) * ROWS].T
    turn_query(jnp.minimum(step + 2, STEPS - 1))

    @pl.when(step < STEPS - 1)
    def _():
        def more(kb, _):
            dqacc[...] += grads(kb)
            return 0

        lax.fori_loop(1, blocks, more, 0)

    @pl.when(step == STEPS - 1)
    def _():
        def stage(kb):
            turned = acc[pl.ds(blk(kb), KB), :].T
            slot = lax.rem(kb, 2)
            for t in range(NY):
                tile = turned[:, t * ROWS:(t + 1) * ROWS].reshape(NXL, NC, PART, ROWS)
                for side in range(NXL):
                    st_f[slot, (t - y) & 3, side ^ xl] = tile[side]
                    st_b[slot, (t - y) & 3, side ^ xl] = tile[side].astype(BF16)

        def room(kb):
            @pl.when(kb >= 2)
            def _():
                deliver_block(kb - 2, end)

        def more(kb, _):
            room(kb - 1)
            stage(kb - 1)
            dqacc[...] += grads(kb)
            deliver_block(kb - 1, begin)
            return 0

        lax.fori_loop(1, blocks, more, 0)
        room(blocks - 1)
        stage(blocks - 1)
        send_dq(step - 2).wait()
        turn_dq(step)
        deliver_block(blocks - 1, begin)
        send_dq(step).start()

        def finish(kb, _):
            deliver_block(kb, end)
            return 0

        lax.fori_loop(jnp.maximum(blocks - 2, 0), blocks, finish, 0)
        for block in range(SEQ // KB):
            clear(block, end)
        send_dq(step - 1).wait()
        send_dq(step).wait()


def attend(segments, query, grad, pieces):
    any_spec = pl.BlockSpec(memory_space=pl.ANY)
    tile = (NY, NXL, PART, ROWS)
    staged = (2, NY, NXL, NC, PART, ROWS)
    rings = (NZ, NY, NXH, NXL, PART, ROWS)
    return pl.pallas_call(
        attend_kernel,
        grid_spec=pltpu.PrefetchScalarGridSpec(
            num_scalar_prefetch=1,
            grid=(STEPS,),
            in_specs=[
                pl.BlockSpec((ROWS, GROUPS * WIDTH), lambda i, s: (0, 0)),
                pl.BlockSpec((ROWS, GROUPS * LATENT), lambda i, s: (0, 0)),
            ] + [any_spec] * 8,
            out_specs=[
                pl.BlockSpec((ROWS, HEADS * LATENT), lambda i, s: (0, i)),
                any_spec,
                any_spec,
                any_spec,
            ],
            scratch_shapes=[
                pltpu.VMEM((SEQ, WIDTH), BF16),
                pltpu.VMEM((WIDTH, SEQ), BF16),
                pltpu.VMEM((MAXB * KB, CHUNK), F32),
                pltpu.VMEM((MAXB * KB, CHUNK), BF16),
                pltpu.VMEM((MAXB * KB, WIDTH), F32),
                pltpu.VMEM((WIDTH, CHUNK), BF16),
                pltpu.VMEM((LATENT, CHUNK), BF16),
                pltpu.VMEM((CHUNK, WIDTH), BF16),
                pltpu.VMEM((CHUNK, LATENT), BF16),
                pltpu.VMEM((8, CHUNK), F32),
                pltpu.VMEM((8, CHUNK), F32),
                pltpu.VMEM((LATENT, CHUNK), F32),
                pltpu.VMEM((WIDTH, CHUNK), F32),
                pltpu.VMEM((2, ROWS, HEADS * WIDTH), F32),
                pltpu.VMEM(staged, F32),
                pltpu.VMEM(staged, BF16),
                pltpu.VMEM(tile, F32),
                pltpu.VMEM(tile, BF16),
                pltpu.SemaphoreType.DMA((SEQ // ROWS, 2)),
                pltpu.SemaphoreType.DMA((2, 2)),
                pltpu.SemaphoreType.DMA((2, SEQ // KB)),
                pltpu.SemaphoreType.DMA((2,)),
            ],
        ),
        out_shape=[
            jax.ShapeDtypeStruct((ROWS, GROUPS * LATENT), F32),
            jax.ShapeDtypeStruct((ROWS, GROUPS * WIDTH), F32),
            jax.ShapeDtypeStruct(rings, F32),
            jax.ShapeDtypeStruct(rings, BF16),
        ],
        compiler_params=pltpu.CompilerParams(
            dimension_semantics=("arbitrary",), vmem_limit_bytes=58 * 1024 * 1024
        ),
        cost_estimate=pl.CostEstimate(
            flops=40 * 10**9, bytes_accessed=30 * 10**6, transcendentals=10**7
        ),
        name="attend",
    )(segments, query, grad, *pieces)


def deliver(keep, out):
    def part(i):
        return keep[i] + send(out[i], other_core).astype(F32)

    def wide(x):
        return x.astype(F32)

    far = send(part(2).astype(BF16), along(0, 1))
    down = send(part(3).astype(BF16), along(0, 3))
    up = send((part(1) + wide(far)).astype(BF16), along(0, 1))
    total = part(0) + wide(up) + wide(down)
    parts = total.astype(BF16)
    ring = [wide(send(parts[d], along(1, d))) for d in (1, 3, 2)]
    total = total[0] + ring[0] + ring[1] + ring[2]
    parts = total.astype(BF16)
    ring = [wide(send(parts[a, b], along_x(a, b))) for a, b in ((0, 1), (1, 1), (1, 0))]
    return total[0, 0] + ring[0] + ring[1] + ring[2]


def shards(query, compressed, segments, grad_attn):
    pieces = collect(compressed, lax.axis_index("head") % NC)
    attended, query_grad, keep, out = attend(segments, query, grad_attn, pieces)
    return attended, query_grad, deliver(keep, out).T


def solution(mesh):
    placed = (P("ctx", "head"), P("ctx", None), P(), P("ctx", "head"))
    return jax.shard_map(
        shards,
        mesh=mesh,
        in_specs=placed,
        out_specs=(P("ctx", "head"), P("ctx", "head"), P("ctx", "head")),
        check_vma=False,
    )
```

```python
import math

import jax
import jax.numpy as jnp
from jax import lax
from jax.experimental import pallas as pl
from jax.experimental.pallas import tpu as pltpu
from jax.sharding import PartitionSpec as P

LATENT = 512
ROPE = 64
WIDTH = LATENT + ROPE
ROWS = 128
GROUPS = 16
LANES = ROWS * GROUPS
SEQ = 4096
HALF = WIDTH // 2
PART = WIDTH // 4
KB = 512
MAXB = 7
HEADS = 4
CHUNK = HEADS * ROWS
STEPS = LANES // CHUNK

SCALE = 1.0 / math.sqrt(192.0)
SCALE2 = SCALE * math.log2(math.e)
NEG = -1e30

NZ, NXH, NY, NXL, NC = 4, 2, 4, 2, 2
F32, BF16 = jnp.float32, jnp.bfloat16


def flat(z, xh, y, xl, c):
    return ((z * NXH + xh) * NY + y) * (NXL * NC) + xl * NC + c


def send(x, move):
    pairs = []
    for z in range(NZ):
        for xh in range(NXH):
            for y in range(NY):
                for xl in range(NXL):
                    for c in range(NC):
                        to = move(z, xh, y, xl, c)
                        pairs.append((flat(z, xh, y, xl, c), flat(*to)))
    return lax.ppermute(x, ("ctx", "head"), pairs)


def other_core(z, xh, y, xl, c):
    return (z, xh, y, xl, 1 - c)


def across_x(z, xh, y, xl, c):
    return (z, 1 - xh, y, 1 - xl, c)


def along_x(dxh, dxl):
    return lambda z, xh, y, xl, c: (z, (xh + dxh) % NXH, y, (xl + dxl) % NXL, c)


def along(axis, d):
    def move(z, xh, y, xl, c):
        if c == axis:
            return ((z + d) % NZ, xh, y, xl, c)
        return (z, xh, (y + d) % NY, xl, c)

    return move


def collect(own, core, query, grad):
    mine = lax.dynamic_slice_in_dim(own.T, core * HALF, HALF, 0)
    pair = jnp.stack([mine, send(mine, across_x)])
    one, three, two = [send(pair, along(1, d)) for d in (1, 3, 2)]
    near, near2 = jnp.stack([pair, one]), jnp.stack([three, two])
    near, near2, query, grad = lax.optimization_barrier((near, near2, query, grad))
    below, above2 = send(near, along(0, 1)), send(near2, along(0, 3))
    below2, above = send(near2, along(0, 1)), send(near, along(0, 3))
    rows = lay_out(query, grad)
    below, above2, near, near2, rows = lax.optimization_barrier(
        (below, above2, near, near2, rows)
    )
    far, far2 = send(below, along(0, 1)), send(above2, along(0, 3))
    pieces = [near, near2, below, below2, above, above2, far, far2]
    return pieces + [send(p, other_core) for p in pieces], rows


RING = (0, -1, 1, 2)


def lay_out_kernel(q_ref, g_ref, qt_ref, gt_ref, qn_ref, gn_ref):
    for x_ref, t_ref, n_ref, width in ((q_ref, qt_ref, qn_ref, WIDTH), (g_ref, gt_ref, gn_ref, LATENT)):
        x = x_ref[...]
        turned = x.T
        for h in range(HEADS):
            rows = slice(h * ROWS, (h + 1) * ROWS)
            t_ref[:, rows] = turned[h * width:(h + 1) * width]
            n_ref[rows, :] = x[:, h * width:(h + 1) * width]


def lay_out(query, grad):
    wide = lambda w: pl.BlockSpec((ROWS, HEADS * w), lambda i: (0, i))
    columns = lambda w: pl.BlockSpec((w, CHUNK), lambda i: (0, i))
    rows = lambda w: pl.BlockSpec((CHUNK, w), lambda i: (i, 0))
    shapes = [(WIDTH, LANES), (LATENT, LANES), (LANES, WIDTH), (LANES, LATENT)]
    return pl.pallas_call(
        lay_out_kernel,
        grid=(STEPS,),
        in_specs=[wide(WIDTH), wide(LATENT)],
        out_specs=[columns(WIDTH), columns(LATENT), rows(WIDTH), rows(LATENT)],
        out_shape=[jax.ShapeDtypeStruct(shape, BF16) for shape in shapes],
        compiler_params=pltpu.CompilerParams(
            dimension_semantics=("arbitrary",), vmem_limit_bytes=60 * 1024 * 1024
        ),
        cost_estimate=pl.CostEstimate(flops=0, bytes_accessed=14 * 10**6, transcendentals=0),
        name="lay_out",
    )(query, grad)


def turn_back_kernel(width, x_ref, out_ref):
    x = x_ref[...]
    out_ref[...] = jnp.concatenate(
        [x[:, h * ROWS:(h + 1) * ROWS] for h in range(HEADS)], axis=0
    ).T


def turn_back(x):
    width = x.shape[0]
    return pl.pallas_call(
        lambda *refs: turn_back_kernel(width, *refs),
        grid=(STEPS,),
        in_specs=[pl.BlockSpec((width, CHUNK), lambda i: (0, i))],
        out_specs=pl.BlockSpec((ROWS, HEADS * width), lambda i: (0, i)),
        out_shape=jax.ShapeDtypeStruct((ROWS, GROUPS * width), F32),
        compiler_params=pltpu.CompilerParams(
            dimension_semantics=("arbitrary",), vmem_limit_bytes=60 * 1024 * 1024
        ),
        cost_estimate=pl.CostEstimate(
            flops=0, bytes_accessed=2 * 4 * width * LANES, transcendentals=0
        ),
        name="turn_back",
    )(x)


def attend_kernel(segments, qt0, qt, gt, qn, gn, *rest):
    pieces = rest[:16]
    o_ref, dq_ref, keep_ref = rest[16:19]
    send_refs = rest[19:27]
    (c_v, ct_v, s_v, w_v, e_v, acc, top_v, total_v, st_f, st_b, zero_f, zero_b, in_sem, out_sem,
     zero_sem) = rest[27:]
    step = pl.program_id(0)
    ctx, head = lax.axis_index("ctx"), lax.axis_index("head")
    z, xh, y, xl, core = ctx >> 3, (ctx >> 2) & 1, ctx & 3, head >> 1, head & 1

    def bound(value):
        def halve(_, ends):
            low, high = ends
            mid = (low + high) >> 1
            less = (low < high) & (segments[jnp.minimum(mid, SEQ - 1)] < value)
            return jnp.where(less, mid + 1, low), jnp.where(less, high, mid)

        return lax.fori_loop(0, 13, halve, (jnp.int32(0), jnp.int32(SEQ)))[0]

    second, third = bound(1), bound(2)

    def start_of(position):
        return jnp.where(position >= third, third, jnp.where(position >= second, second, 0))

    first_row = ctx * ROWS
    first = start_of(first_row) // KB
    blocks = (first_row + ROWS + KB - 1) // KB - first
    free_low, free_high = start_of(first_row + ROWS - 1), first_row + 1
    token = first_row + (lax.broadcasted_iota(jnp.int32, (1, CHUNK), 1) & (ROWS - 1))
    start = start_of(token)

    def off(kb):
        return pl.multiple_of((first + kb) * KB, KB)

    def blk(kb):
        return pl.multiple_of(kb * KB, KB)

    def live(block):
        return (block >= first) & (block < first + blocks)

    def fetch(piece, to, half):
        return pltpu.make_async_copy(
            piece,
            ct_v.at[
                pl.ds(pl.multiple_of(half * HALF, 32), HALF),
                pl.ds(pl.multiple_of((to - first * (KB // ROWS)) * ROWS, ROWS), ROWS),
            ],
            in_sem.at[to, half],
        )

    def fetch_all():
        for n in range(64):
            other, piece, side, slot, x = n // 32, n // 8 % 4, n // 4 % 2, n // 2 % 2, n % 2
            half = 1 - core if other else core
            one, two = RING[2 * side + slot], RING[piece]
            dy = jnp.where(half == 0, one, two)
            dz = jnp.where(half == 0, two, one)
            to = ((z + dz) & 3) * 8 + (xh ^ x) * 4 + ((y + dy) & 3)

            @pl.when(live(to >> 2))
            def _():
                fetch(pieces[other * 8 + piece * 2 + side].at[slot, x], to, half).start()

    def by_core(act):
        for c in range(NC):
            @pl.when(core == c)
            def _():
                act(c)

    def hand_out(block, kept, sent, sems, act):
        dz, x = ((block >> 1) - z) & 3, (block & 1) ^ xh

        def copies(c):
            ref = keep_ref.at[dz, :, x] if c == 0 else keep_ref.at[:, dz, x]
            act(pltpu.make_async_copy(kept(c), ref, sems.at[0]))
            for i, send_ref in enumerate(send_refs):
                r, half = i // 2, i % 2
                if c == 1:
                    @pl.when(dz == r)
                    def _():
                        tiles = sent(0).at[pl.ds(2 * half, 2)]
                        act(pltpu.make_async_copy(tiles, send_ref.at[:, x], sems.at[1 + i]))
                else:
                    @pl.when(dz >> 1 == half)
                    def _():
                        place = send_ref.at[dz & 1, x]
                        act(pltpu.make_async_copy(sent(1).at[r], place, sems.at[1 + i]))

        by_core(copies)

    def clear(block, act):
        @pl.when(jnp.logical_not(live(block)))
        def _():
            hand_out(block, lambda c: zero_f, lambda c: zero_b, zero_sem.at[block], act)

    def deliver_block(kb, act):
        slot = lax.rem(kb, 2)
        hand_out(
            first + kb, lambda c: st_f.at[slot, :, :, c], lambda c: st_b.at[slot, :, :, c],
            out_sem.at[slot], act,
        )

    def begin(copy):
        copy.start()

    def end(copy):
        copy.wait()

    def score(kb, masked, q):
        s = jnp.dot(c_v[pl.ds(blk(kb), KB), :], q[...], preferred_element_type=F32)
        if masked:
            key = off(kb) + lax.broadcasted_iota(jnp.int32, (KB, CHUNK), 0)
            s = jnp.where((key >= start) & (key <= token), s, NEG)
        return s

    def folded(x):
        return x.reshape(KB // 8, 8, CHUNK)

    def keep_score(kb, s, top):
        s_v[pl.ds(blk(kb), KB), :] = s
        return jnp.maximum(top, jnp.max(folded(s), axis=0))

    lowest = jnp.full((8, CHUNK), NEG, F32)

    @pl.when(step == 0)
    def _():
        fetch_all()
        zero_f[...] = jnp.zeros_like(zero_f)
        zero_b[...] = jnp.zeros_like(zero_b)
        for block in range(SEQ // KB):
            clear(block, begin)

        def turn(kb, top):
            for t in range(KB // ROWS):
                for half in range(2):
                    fetch(pieces[0].at[0, 0], (first + kb) * (KB // ROWS) + t, half).wait()
            c_v[pl.ds(blk(kb), KB), :] = ct_v[:, pl.ds(blk(kb), KB)].T
            acc[pl.ds(blk(kb), KB), :] = jnp.zeros((KB, WIDTH), F32)
            return keep_score(kb, score(kb, True, qt0), top)

        top_v[...] = lax.fori_loop(0, blocks, turn, lowest)

    top = jnp.max(top_v[...], axis=0, keepdims=True)

    def sweep(body, carried):
        pairs = (blocks - 1) // 2
        carried = lax.fori_loop(0, pairs, lambda i, c: body(2 * i + 1, 2, c), carried)
        return lax.fori_loop(2 * pairs + 1, blocks, lambda i, c: body(i, 1, c), carried)

    def values(kb, n):
        total = jnp.zeros((8, CHUNK), F32)
        for i in [kb + i for i in range(n)]:
            rows = pl.ds(blk(i), KB)
            w_v[rows, :] = jnp.dot(
                c_v[pl.ds(blk(i), KB), :LATENT], gt[...], preferred_element_type=F32
            )
            e = jnp.exp2((s_v[rows, :] - top) * SCALE2)
            total = total + folded(e).sum(axis=0)
            e_v[rows, :] = e.astype(BF16)
        return total, jnp.dot(
            ct_v[:LATENT, pl.ds(blk(kb), n * KB)], e_v[pl.ds(blk(kb), n * KB), :],
            preferred_element_type=F32,
        )

    total, out = values(0, 1)
    o_ref[...] = out

    def more_values(kb, n, total):
        added, out = values(kb, n)
        o_ref[...] += out
        return total + added

    total_v[...] = sweep(more_values, total)

    inverse = 1.0 / jnp.sum(total_v[...], axis=0, keepdims=True)
    out = o_ref[...] * inverse
    o_ref[...] = out
    dots = jnp.sum(gt[...].astype(F32) * out, axis=0, keepdims=True)

    def grads(kb, n, masked, top):
        ds = [None] * n
        s = [None] * n

        def weigh(i):
            rows = pl.ds(blk(kb + i), KB)
            p = e_v[rows, :].astype(F32) * inverse
            ds[i] = (p * (w_v[rows, :] - dots) * SCALE).astype(BF16)
            return p.astype(BF16)

        def add(i, p):
            rows = pl.ds(blk(kb + i), KB)
            dv = jnp.dot(p, gn[...], preferred_element_type=F32)
            dk = jnp.dot(ds[i], qn[...], preferred_element_type=F32)
            acc[rows, :LATENT] += dk[:, :LATENT] + dv
            acc[rows, LATENT:] += dk[:, LATENT:]

        ahead = masked is not None
        if ahead:
            s[0] = score(kb, masked, qt)
        p = weigh(0)
        for i in range(n):
            if ahead and i + 1 < n:
                s[i + 1] = score(kb + i + 1, masked, qt)
            add(i, p)
            if i + 1 < n:
                p = weigh(i + 1)
            if ahead:
                top = keep_score(kb + i, s[i], top)
        ds = ds[0] if n == 1 else jnp.concatenate(ds, axis=0)
        dq = jnp.dot(ct_v[:, pl.ds(blk(kb), n * KB)], ds, preferred_element_type=F32)
        return dq, top

    @pl.when(step < STEPS - 1)
    def _():
        dq, above = grads(0, 1, True, lowest)
        dq_ref[...] = dq

        def more(kb, n, above):
            def body(masked):
                def run(above):
                    dq, above = grads(kb, n, masked, above)
                    dq_ref[...] += dq
                    return above

                return run

            free = (off(kb) >= free_low) & (off(kb) + n * KB <= free_high)
            return lax.cond(free, body(False), body(True), above)

        top_v[...] = sweep(more, above)

    @pl.when(step == STEPS - 1)
    def _():
        dq_ref[...] = grads(0, 1, None, None)[0]

        def stage(kb):
            turned = acc[pl.ds(blk(kb), KB), :].T
            slot = lax.rem(kb, 2)
            for t in range(NY):
                tile = turned[:, t * ROWS:(t + 1) * ROWS].reshape(NXL, NC, PART, ROWS)
                for side in range(NXL):
                    st_f[slot, (t - y) & 3, side ^ xl] = tile[side]
                    st_b[slot, (t - y) & 3, side ^ xl] = tile[side].astype(BF16)

        def room(kb):
            @pl.when(kb >= 2)
            def _():
                deliver_block(kb - 2, end)

        def more(kb, _):
            room(kb - 1)
            stage(kb - 1)
            dq_ref[...] += grads(kb, 1, None, None)[0]
            deliver_block(kb - 1, begin)
            return 0

        lax.fori_loop(1, blocks, more, 0)
        room(blocks - 1)
        stage(blocks - 1)
        deliver_block(blocks - 1, begin)

        def finish(kb, _):
            deliver_block(kb, end)
            return 0

        lax.fori_loop(jnp.maximum(blocks - 2, 0), blocks, finish, 0)
        for block in range(SEQ // KB):
            clear(block, end)


def attend(segments, qt, gt, qn, gn, pieces):
    any_spec = pl.BlockSpec(memory_space=pl.ANY)
    tile = (NY, NXL, PART, ROWS)
    staged = (2, NY, NXL, NC, PART, ROWS)
    rings = (NZ, NY, NXH, NXL, PART, ROWS)
    return pl.pallas_call(
        attend_kernel,
        grid_spec=pltpu.PrefetchScalarGridSpec(
            num_scalar_prefetch=1,
            grid=(STEPS,),
            in_specs=[
                pl.BlockSpec((WIDTH, CHUNK), lambda i, s: (0, 0)),
                pl.BlockSpec((WIDTH, CHUNK), lambda i, s: (0, jnp.minimum(i + 1, STEPS - 1))),
                pl.BlockSpec((LATENT, CHUNK), lambda i, s: (0, i)),
                pl.BlockSpec((CHUNK, WIDTH), lambda i, s: (i, 0)),
                pl.BlockSpec((CHUNK, LATENT), lambda i, s: (i, 0)),
            ] + [any_spec] * 16,
            out_specs=[
                pl.BlockSpec((LATENT, CHUNK), lambda i, s: (0, i)),
                pl.BlockSpec((WIDTH, CHUNK), lambda i, s: (0, i)),
            ] + [any_spec] * 9,
            scratch_shapes=[
                pltpu.VMEM((MAXB * KB, WIDTH), BF16),
                pltpu.VMEM((WIDTH, MAXB * KB), BF16),
                pltpu.VMEM((MAXB * KB, CHUNK), F32),
                pltpu.VMEM((MAXB * KB, CHUNK), F32),
                pltpu.VMEM((MAXB * KB, CHUNK), BF16),
                pltpu.VMEM((MAXB * KB, WIDTH), F32),
                pltpu.VMEM((8, CHUNK), F32),
                pltpu.VMEM((8, CHUNK), F32),
                pltpu.VMEM(staged, F32),
                pltpu.VMEM(staged, BF16),
                pltpu.VMEM(tile, F32),
                pltpu.VMEM(tile, BF16),
                pltpu.SemaphoreType.DMA((SEQ // ROWS, 2)),
                pltpu.SemaphoreType.DMA((2, 9)),
                pltpu.SemaphoreType.DMA((SEQ // KB, 9)),
            ],
        ),
        out_shape=[
            jax.ShapeDtypeStruct((LATENT, LANES), F32),
            jax.ShapeDtypeStruct((WIDTH, LANES), F32),
            jax.ShapeDtypeStruct(rings, F32),
        ] + [jax.ShapeDtypeStruct((2,) + rings[2:], BF16)] * 8,
        compiler_params=pltpu.CompilerParams(
            dimension_semantics=("arbitrary",), vmem_limit_bytes=60 * 1024 * 1024
        ),
        cost_estimate=pl.CostEstimate(
            flops=40 * 10**9, bytes_accessed=30 * 10**6, transcendentals=10**7
        ),
        name="attend",
    )(segments, qt, qt, gt, qn, gn, *pieces)


def deliver(keep, out, attended, query_grad):
    def part(i, half):
        mine = keep[i, 2 * half:2 * half + 2]
        return mine + wide(send(out[2 * i + half], other_core))

    def wide(x):
        return x.astype(F32)

    def ring(x, axis, d):
        return wide(send(x.astype(BF16), along(axis, d)))

    far, far2 = part(2, 0).astype(BF16), part(2, 1).astype(BF16)
    far, far2, *late = lax.optimization_barrier((far, far2, out[0], out[1], out[2], out[7]))
    out = [*late[:3], *out[3:7], late[3]]
    far, far2 = ring(far, 0, 1), ring(far2, 0, 3)
    up2, down = ring(part(1, 1), 0, 1), ring(part(3, 0), 0, 3)
    up, down2 = (part(1, 0) + far).astype(BF16), (part(3, 1) + far2).astype(BF16)
    up, down2, attended = lax.optimization_barrier((up, down2, attended))
    up, down2 = ring(up, 0, 1), ring(down2, 0, 3)
    attended = turn_back(attended)
    near = part(0, 0) + up + down
    near2 = part(0, 1) + up2 + down2
    parts = near[1].astype(BF16), near2[0].astype(BF16), near2[1].astype(BF16)
    *parts, attended, query_grad = lax.optimization_barrier((*parts, attended, query_grad))
    total = near[0] + ring(parts[0], 1, 1) + ring(parts[1], 1, 2) + ring(parts[2], 1, 3)
    query_grad = turn_back(query_grad)
    parts, query_grad = lax.optimization_barrier((total.astype(BF16), query_grad))
    got = [wide(send(parts[a, b], along_x(a, b))) for a, b in ((0, 1), (1, 1), (1, 0))]
    return attended, query_grad, (total[0, 0] + got[0] + got[1] + got[2]).T


def shards(query, compressed, segments, grad_attn):
    pieces, rows = collect(compressed, lax.axis_index("head") % NC, query, grad_attn)
    attended, query_grad, keep, *out = attend(segments, *rows, pieces)
    return deliver(keep, out, attended, query_grad)


def solution(mesh):
    placed = (P("ctx", "head"), P("ctx", None), P(), P("ctx", "head"))
    return jax.shard_map(
        shards,
        mesh=mesh,
        in_specs=placed,
        out_specs=(P("ctx", "head"), P("ctx", "head"), P("ctx", "head")),
        check_vma=False,
    )
```

```python
import math

import jax
import jax.numpy as jnp
from jax import lax
from jax.experimental import pallas as pl
from jax.experimental.pallas import tpu as pltpu
from jax.sharding import PartitionSpec as P

LATENT = 512
ROPE = 64
WIDTH = LATENT + ROPE
ROWS = 128
GROUPS = 16
LANES = ROWS * GROUPS
SEQ = 4096
HALF = WIDTH // 2
PART = WIDTH // 4
KB = 512
MAXB = 7
HEADS = 4
CHUNK = HEADS * ROWS
STEPS = LANES // CHUNK

SCALE = 1.0 / math.sqrt(192.0)
NEG = -1e30

NZ, NXH, NY, NXL, NC = 4, 2, 4, 2, 2
F32, BF16 = jnp.float32, jnp.bfloat16


def flat(z, xh, y, xl, c):
    return ((z * NXH + xh) * NY + y) * (NXL * NC) + xl * NC + c


def send(x, move):
    pairs = []
    for z in range(NZ):
        for xh in range(NXH):
            for y in range(NY):
                for xl in range(NXL):
                    for c in range(NC):
                        to = move(z, xh, y, xl, c)
                        pairs.append((flat(z, xh, y, xl, c), flat(*to)))
    return lax.ppermute(x, ("ctx", "head"), pairs)


def other_core(z, xh, y, xl, c):
    return (z, xh, y, xl, 1 - c)


def across_x(z, xh, y, xl, c):
    return (z, 1 - xh, y, 1 - xl, c)


def along_x(dxh, dxl):
    return lambda z, xh, y, xl, c: (z, (xh + dxh) % NXH, y, (xl + dxl) % NXL, c)


def along(axis, d):
    def move(z, xh, y, xl, c):
        if c == axis:
            return ((z + d) % NZ, xh, y, xl, c)
        return (z, xh, (y + d) % NY, xl, c)

    return move


def collect(own, core, query, grad):
    mine = lax.dynamic_slice_in_dim(own.T, core * HALF, HALF, 0)
    pair = jnp.stack([mine, send(mine, across_x)])
    near = jnp.stack([pair] + [send(pair, along(1, d)) for d in (1, 3, 2)])
    near, query, grad = lax.optimization_barrier((near, query, grad))
    below, above = send(near, along(0, 1)), send(near, along(0, 3))
    below, rows = lax.optimization_barrier((below, lay_out(query, grad)))
    pieces = [near, below, above, send(below, along(0, 1))]
    return pieces + [send(p, other_core) for p in pieces], rows


RING = (0, -1, 1, 2)


def lay_out_kernel(q_ref, g_ref, qt_ref, gt_ref, qn_ref, gn_ref):
    for x_ref, t_ref, n_ref, width in ((q_ref, qt_ref, qn_ref, WIDTH), (g_ref, gt_ref, gn_ref, LATENT)):
        x = x_ref[...]
        turned = x.T
        for h in range(HEADS):
            rows = slice(h * ROWS, (h + 1) * ROWS)
            t_ref[:, rows] = turned[h * width:(h + 1) * width]
            n_ref[rows, :] = x[:, h * width:(h + 1) * width]


def lay_out(query, grad):
    wide = lambda w: pl.BlockSpec((ROWS, HEADS * w), lambda i: (0, i))
    columns = lambda w: pl.BlockSpec((w, CHUNK), lambda i: (0, i))
    rows = lambda w: pl.BlockSpec((CHUNK, w), lambda i: (i, 0))
    shapes = [(WIDTH, LANES), (LATENT, LANES), (LANES, WIDTH), (LANES, LATENT)]
    return pl.pallas_call(
        lay_out_kernel,
        grid=(STEPS,),
        in_specs=[wide(WIDTH), wide(LATENT)],
        out_specs=[columns(WIDTH), columns(LATENT), rows(WIDTH), rows(LATENT)],
        out_shape=[jax.ShapeDtypeStruct(shape, BF16) for shape in shapes],
        compiler_params=pltpu.CompilerParams(
            dimension_semantics=("arbitrary",), vmem_limit_bytes=60 * 1024 * 1024
        ),
        cost_estimate=pl.CostEstimate(flops=0, bytes_accessed=14 * 10**6, transcendentals=0),
        name="lay_out",
    )(query, grad)


def turn_back_kernel(width, x_ref, out_ref):
    x = x_ref[...]
    out_ref[...] = jnp.concatenate(
        [x[:, h * ROWS:(h + 1) * ROWS] for h in range(HEADS)], axis=0
    ).T


def turn_back(x):
    width = x.shape[0]
    return pl.pallas_call(
        lambda *refs: turn_back_kernel(width, *refs),
        grid=(STEPS,),
        in_specs=[pl.BlockSpec((width, CHUNK), lambda i: (0, i))],
        out_specs=pl.BlockSpec((ROWS, HEADS * width), lambda i: (0, i)),
        out_shape=jax.ShapeDtypeStruct((ROWS, GROUPS * width), F32),
        compiler_params=pltpu.CompilerParams(
            dimension_semantics=("arbitrary",), vmem_limit_bytes=60 * 1024 * 1024
        ),
        cost_estimate=pl.CostEstimate(
            flops=0, bytes_accessed=2 * 4 * width * LANES, transcendentals=0
        ),
        name="turn_back",
    )(x)


def attend_kernel(segments, qt0, qt, gt, qn, gn, *rest):
    pieces = rest[:8]
    o_ref, dq_ref, keep_ref = rest[8:11]
    send_refs = rest[11:15]
    (c_v, ct_v, s_v, w_v, e_v, acc, top_v, total_v, st_f, st_b, zero_f, zero_b, in_sem, out_sem,
     zero_sem, bounds) = rest[15:]
    step = pl.program_id(0)
    ctx, head = lax.axis_index("ctx"), lax.axis_index("head")
    z, xh, y, xl, core = ctx >> 3, (ctx >> 2) & 1, ctx & 3, head >> 1, head & 1

    @pl.when(step == 0)
    def _():
        def halve(_, ends):
            found = []
            for value, (low, high) in zip((1, 2), ends):
                mid = (low + high) >> 1
                less = (low < high) & (segments[jnp.minimum(mid, SEQ - 1)] < value)
                found.append((jnp.where(less, mid + 1, low), jnp.where(less, high, mid)))
            return tuple(found)

        ends = (jnp.int32(0), jnp.int32(SEQ))
        ends = lax.fori_loop(0, 13, halve, (ends, ends))
        bounds[0], bounds[1] = ends[0][0], ends[1][0]

    second, third = bounds[0], bounds[1]

    def start_of(position):
        return jnp.where(position >= third, third, jnp.where(position >= second, second, 0))

    first_row = ctx * ROWS
    first = start_of(first_row) // KB
    blocks = (first_row + ROWS + KB - 1) // KB - first
    free_low, free_high = start_of(first_row + ROWS - 1), first_row + 1
    token = first_row + (lax.broadcasted_iota(jnp.int32, (1, CHUNK), 1) & (ROWS - 1))
    start = start_of(token)

    def off(kb):
        return pl.multiple_of((first + kb) * KB, KB)

    def blk(kb):
        return pl.multiple_of(kb * KB, KB)

    def live(block):
        return (block >= first) & (block < first + blocks)

    def fetch(piece, to, half):
        return pltpu.make_async_copy(
            piece,
            ct_v.at[
                pl.ds(pl.multiple_of(half * HALF, 32), HALF),
                pl.ds(pl.multiple_of((to - first * (KB // ROWS)) * ROWS, ROWS), ROWS),
            ],
            in_sem.at[to, half],
        )

    def fetch_all():
        for n in range(64):
            other, piece, slot, x = n // 32, n // 8 % 4, n // 2 % 4, n % 2
            half = 1 - core if other else core
            dy = jnp.where(half == 0, RING[slot], RING[piece])
            dz = jnp.where(half == 0, RING[piece], RING[slot])
            to = ((z + dz) & 3) * 8 + (xh ^ x) * 4 + ((y + dy) & 3)

            @pl.when(live(to >> 2))
            def _():
                fetch(pieces[other * 4 + piece].at[slot, x], to, half).start()

    def by_core(act):
        for c in range(NC):
            @pl.when(core == c)
            def _():
                act(c)

    def hand_out(block, kept, sent, sems, act):
        dz, x = ((block >> 1) - z) & 3, (block & 1) ^ xh

        def copies(c):
            ref = keep_ref.at[dz, :, x] if c == 0 else keep_ref.at[:, dz, x]
            act(pltpu.make_async_copy(kept(c), ref, sems.at[0]))
            for r, send_ref in enumerate(send_refs):
                if c == 1:
                    @pl.when(dz == r)
                    def _():
                        act(pltpu.make_async_copy(sent(0), send_ref.at[:, x], sems.at[1 + r]))
                else:
                    act(pltpu.make_async_copy(sent(1).at[r], send_ref.at[dz, x], sems.at[1 + r]))

        by_core(copies)

    def clear(block, act):
        @pl.when(jnp.logical_not(live(block)))
        def _():
            hand_out(block, lambda c: zero_f, lambda c: zero_b, zero_sem.at[block], act)

    def deliver_block(kb, act):
        slot = lax.rem(kb, 2)
        hand_out(
            first + kb, lambda c: st_f.at[slot, :, :, c], lambda c: st_b.at[slot, :, :, c],
            out_sem.at[slot], act,
        )

    def begin(copy):
        copy.start()

    def end(copy):
        copy.wait()

    def score(kb, masked, q):
        s = jnp.dot(c_v[pl.ds(blk(kb), KB), :], q[...], preferred_element_type=F32)
        if masked:
            key = off(kb) + lax.broadcasted_iota(jnp.int32, (KB, CHUNK), 0)
            s = jnp.where((key >= start) & (key <= token), s, NEG)
        return s

    def folded(x):
        return x.reshape(KB // 8, 8, CHUNK)

    def keep_score(kb, s, top):
        s_v[pl.ds(blk(kb), KB), :] = s
        return jnp.maximum(top, jnp.max(folded(s), axis=0))

    lowest = jnp.full((8, CHUNK), NEG, F32)

    @pl.when(step == 0)
    def _():
        fetch_all()
        zero_f[...] = jnp.zeros_like(zero_f)
        zero_b[...] = jnp.zeros_like(zero_b)
        for block in range(SEQ // KB):
            clear(block, begin)

        def turn(kb, top):
            for t in range(KB // ROWS):
                for half in range(2):
                    fetch(pieces[0].at[0, 0], (first + kb) * (KB // ROWS) + t, half).wait()
            c_v[pl.ds(blk(kb), KB), :] = ct_v[:, pl.ds(blk(kb), KB)].T
            acc[pl.ds(blk(kb), KB), :] = jnp.zeros((KB, WIDTH), F32)
            return keep_score(kb, score(kb, True, qt0), top)

        top_v[...] = lax.fori_loop(0, blocks, turn, lowest)

    top = jnp.max(top_v[...], axis=0, keepdims=True)

    def sweep(body, carried):
        pairs = (blocks - 1) // 2
        carried = lax.fori_loop(0, pairs, lambda i, c: body(2 * i + 1, 2, c), carried)
        return lax.fori_loop(2 * pairs + 1, blocks, lambda i, c: body(i, 1, c), carried)

    def values(kb, n):
        total = jnp.zeros((8, CHUNK), F32)
        for i in [kb + i for i in range(n)]:
            rows = pl.ds(blk(i), KB)
            w_v[rows, :] = jnp.dot(
                c_v[pl.ds(blk(i), KB), :LATENT], gt[...], preferred_element_type=F32
            )
            e = jnp.exp((s_v[rows, :] - top) * SCALE)
            total = total + folded(e).sum(axis=0)
            e_v[rows, :] = e.astype(BF16)
        return total, jnp.dot(
            ct_v[:LATENT, pl.ds(blk(kb), n * KB)], e_v[pl.ds(blk(kb), n * KB), :],
            preferred_element_type=F32,
        )

    total, out = values(0, 1)
    o_ref[...] = out

    def more_values(kb, n, total):
        added, out = values(kb, n)
        o_ref[...] += out
        return total + added

    total_v[...] = sweep(more_values, total)

    inverse = 1.0 / jnp.sum(total_v[...], axis=0, keepdims=True)
    out = o_ref[...] * inverse
    o_ref[...] = out
    dots = jnp.sum(gt[...].astype(F32) * out, axis=0, keepdims=True)

    def grads(kb, n, masked, top):
        ds = [None] * n
        s = [None] * n

        def weigh(i):
            rows = pl.ds(blk(kb + i), KB)
            p = e_v[rows, :].astype(F32) * inverse
            ds[i] = (p * (w_v[rows, :] - dots) * SCALE).astype(BF16)
            return p.astype(BF16)

        def add(i, p):
            rows = pl.ds(blk(kb + i), KB)
            dv = jnp.dot(p, gn[...], preferred_element_type=F32)
            dk = jnp.dot(ds[i], qn[...], preferred_element_type=F32)
            acc[rows, :LATENT] += dk[:, :LATENT] + dv
            acc[rows, LATENT:] += dk[:, LATENT:]

        ahead = masked is not None
        if ahead:
            s[0] = score(kb, masked, qt)
        p = weigh(0)
        for i in range(n):
            if ahead and i + 1 < n:
                s[i + 1] = score(kb + i + 1, masked, qt)
            add(i, p)
            if i + 1 < n:
                p = weigh(i + 1)
            if ahead:
                top = keep_score(kb + i, s[i], top)
        ds = ds[0] if n == 1 else jnp.concatenate(ds, axis=0)
        dq = jnp.dot(ct_v[:, pl.ds(blk(kb), n * KB)], ds, preferred_element_type=F32)
        return dq, top

    @pl.when(step < STEPS - 1)
    def _():
        dq, above = grads(0, 1, True, lowest)
        dq_ref[...] = dq

        def more(kb, n, above):
            def body(masked):
                def run(above):
                    dq, above = grads(kb, n, masked, above)
                    dq_ref[...] += dq
                    return above

                return run

            free = (off(kb) >= free_low) & (off(kb) + n * KB <= free_high)
            return lax.cond(free, body(False), body(True), above)

        top_v[...] = sweep(more, above)

    @pl.when(step == STEPS - 1)
    def _():
        dq_ref[...] = grads(0, 1, None, None)[0]

        def stage(kb):
            turned = acc[pl.ds(blk(kb), KB), :].T
            slot = lax.rem(kb, 2)
            for t in range(NY):
                tile = turned[:, t * ROWS:(t + 1) * ROWS].reshape(NXL, NC, PART, ROWS)
                for side in range(NXL):
                    st_f[slot, (t - y) & 3, side ^ xl] = tile[side]
                    st_b[slot, (t - y) & 3, side ^ xl] = tile[side].astype(BF16)

        def room(kb):
            @pl.when(kb >= 2)
            def _():
                deliver_block(kb - 2, end)

        def more(kb, _):
            room(kb - 1)
            stage(kb - 1)
            dq_ref[...] += grads(kb, 1, None, None)[0]
            deliver_block(kb - 1, begin)
            return 0

        lax.fori_loop(1, blocks, more, 0)
        room(blocks - 1)
        stage(blocks - 1)
        deliver_block(blocks - 1, begin)

        def finish(kb, _):
            deliver_block(kb, end)
            return 0

        lax.fori_loop(jnp.maximum(blocks - 2, 0), blocks, finish, 0)
        for block in range(SEQ // KB):
            clear(block, end)


def attend(segments, qt, gt, qn, gn, pieces):
    any_spec = pl.BlockSpec(memory_space=pl.ANY)
    tile = (NY, NXL, PART, ROWS)
    staged = (2, NY, NXL, NC, PART, ROWS)
    rings = (NZ, NY, NXH, NXL, PART, ROWS)
    return pl.pallas_call(
        attend_kernel,
        grid_spec=pltpu.PrefetchScalarGridSpec(
            num_scalar_prefetch=1,
            grid=(STEPS,),
            in_specs=[
                pl.BlockSpec((WIDTH, CHUNK), lambda i, s: (0, 0)),
                pl.BlockSpec((WIDTH, CHUNK), lambda i, s: (0, jnp.minimum(i + 1, STEPS - 1))),
                pl.BlockSpec((LATENT, CHUNK), lambda i, s: (0, i)),
                pl.BlockSpec((CHUNK, WIDTH), lambda i, s: (i, 0)),
                pl.BlockSpec((CHUNK, LATENT), lambda i, s: (i, 0)),
            ] + [any_spec] * 8,
            out_specs=[
                pl.BlockSpec((LATENT, CHUNK), lambda i, s: (0, i)),
                pl.BlockSpec((WIDTH, CHUNK), lambda i, s: (0, i)),
            ] + [any_spec] * 5,
            scratch_shapes=[
                pltpu.VMEM((MAXB * KB, WIDTH), BF16),
                pltpu.VMEM((WIDTH, MAXB * KB), BF16),
                pltpu.VMEM((MAXB * KB, CHUNK), F32),
                pltpu.VMEM((MAXB * KB, CHUNK), F32),
                pltpu.VMEM((MAXB * KB, CHUNK), BF16),
                pltpu.VMEM((MAXB * KB, WIDTH), F32),
                pltpu.VMEM((8, CHUNK), F32),
                pltpu.VMEM((8, CHUNK), F32),
                pltpu.VMEM(staged, F32),
                pltpu.VMEM(staged, BF16),
                pltpu.VMEM(tile, F32),
                pltpu.VMEM(tile, BF16),
                pltpu.SemaphoreType.DMA((SEQ // ROWS, 2)),
                pltpu.SemaphoreType.DMA((2, 5)),
                pltpu.SemaphoreType.DMA((SEQ // KB, 5)),
                pltpu.SMEM((2,), jnp.int32),
            ],
        ),
        out_shape=[
            jax.ShapeDtypeStruct((LATENT, LANES), F32),
            jax.ShapeDtypeStruct((WIDTH, LANES), F32),
            jax.ShapeDtypeStruct(rings, F32),
        ] + [jax.ShapeDtypeStruct(rings[1:], BF16)] * 4,
        compiler_params=pltpu.CompilerParams(
            dimension_semantics=("arbitrary",), vmem_limit_bytes=60 * 1024 * 1024
        ),
        cost_estimate=pl.CostEstimate(
            flops=40 * 10**9, bytes_accessed=30 * 10**6, transcendentals=10**7
        ),
        name="attend",
    )(segments, qt, qt, gt, qn, gn, *pieces)


def deliver(keep, out, attended, query_grad):
    def part(i):
        return keep[i] + send(out[i], other_core).astype(F32)

    def wide(x):
        return x.astype(F32)

    far, attended = lax.optimization_barrier((part(2).astype(BF16), attended))
    far = send(far, along(0, 1))
    attended = turn_back(attended)
    below = part(3).astype(BF16)
    up = (part(1) + wide(far)).astype(BF16)
    up, attended, query_grad = lax.optimization_barrier((up, attended, query_grad))
    up, down = send(up, along(0, 1)), send(below, along(0, 3))
    query_grad = turn_back(query_grad)
    total = part(0) + wide(up) + wide(down)
    parts, query_grad = lax.optimization_barrier((total.astype(BF16), query_grad))
    ring = [wide(send(parts[d], along(1, d))) for d in (1, 3, 2)]
    total = total[0] + ring[0] + ring[1] + ring[2]
    parts = total.astype(BF16)
    ring = [wide(send(parts[a, b], along_x(a, b))) for a, b in ((0, 1), (1, 1), (1, 0))]
    return attended, query_grad, (total[0, 0] + ring[0] + ring[1] + ring[2]).T


def shards(query, compressed, segments, grad_attn):
    pieces, rows = collect(compressed, lax.axis_index("head") % NC, query, grad_attn)
    attended, query_grad, keep, *out = attend(segments, *rows, pieces)
    return deliver(keep, out, attended, query_grad)


def solution(mesh):
    placed = (P("ctx", "head"), P("ctx", None), P(), P("ctx", "head"))
    return jax.shard_map(
        shards,
        mesh=mesh,
        in_specs=placed,
        out_specs=(P("ctx", "head"), P("ctx", "head"), P("ctx", "head")),
        check_vma=False,
    )
```

```python
import math

import jax
import jax.numpy as jnp
from jax import lax
from jax.experimental import pallas as pl
from jax.experimental.pallas import tpu as pltpu
from jax.sharding import PartitionSpec as P

LATENT = 512
ROPE = 64
WIDTH = LATENT + ROPE
ROWS = 128
GROUPS = 16
LANES = ROWS * GROUPS
SEQ = 4096
HALF = WIDTH // 2
PART = WIDTH // 4
KB = 512
MAXB = 7
HEADS = 4
CHUNK = HEADS * ROWS
STEPS = LANES // CHUNK

SCALE = 1.0 / math.sqrt(192.0)
NEG = -1e30

NZ, NXH, NY, NXL, NC = 4, 2, 4, 2, 2
F32, BF16 = jnp.float32, jnp.bfloat16


def flat(z, xh, y, xl, c):
    return ((z * NXH + xh) * NY + y) * (NXL * NC) + xl * NC + c


def send(x, move):
    pairs = []
    for z in range(NZ):
        for xh in range(NXH):
            for y in range(NY):
                for xl in range(NXL):
                    for c in range(NC):
                        to = move(z, xh, y, xl, c)
                        pairs.append((flat(z, xh, y, xl, c), flat(*to)))
    return lax.ppermute(x, ("ctx", "head"), pairs)


def other_core(z, xh, y, xl, c):
    return (z, xh, y, xl, 1 - c)


def across_x(z, xh, y, xl, c):
    return (z, 1 - xh, y, 1 - xl, c)


def along_x(dxh, dxl):
    return lambda z, xh, y, xl, c: (z, (xh + dxh) % NXH, y, (xl + dxl) % NXL, c)


def along(axis, d):
    def move(z, xh, y, xl, c):
        if c == axis:
            return ((z + d) % NZ, xh, y, xl, c)
        return (z, xh, (y + d) % NY, xl, c)

    return move


def collect(own, core, query, grad):
    mine = lax.dynamic_slice_in_dim(own.T, core * HALF, HALF, 0)
    pair = jnp.stack([mine, send(mine, across_x)])
    near = jnp.stack([pair] + [send(pair, along(1, d)) for d in (1, 3, 2)])
    near, query, grad = lax.optimization_barrier((near, query, grad))
    below, above = send(near, along(0, 1)), send(near, along(0, 3))
    below, rows = lax.optimization_barrier((below, lay_out(query, grad)))
    pieces = [near, below, above, send(below, along(0, 1))]
    return pieces + [send(p, other_core) for p in pieces], rows


RING = (0, -1, 1, 2)


def lay_out_kernel(q_ref, g_ref, qt_ref, gt_ref, qn_ref, gn_ref):
    for x_ref, t_ref, n_ref, width in ((q_ref, qt_ref, qn_ref, WIDTH), (g_ref, gt_ref, gn_ref, LATENT)):
        x = x_ref[...]
        turned = x.T
        for h in range(HEADS):
            rows = slice(h * ROWS, (h + 1) * ROWS)
            t_ref[:, rows] = turned[h * width:(h + 1) * width]
            n_ref[rows, :] = x[:, h * width:(h + 1) * width]


def lay_out(query, grad):
    wide = lambda w: pl.BlockSpec((ROWS, HEADS * w), lambda i: (0, i))
    columns = lambda w: pl.BlockSpec((w, CHUNK), lambda i: (0, i))
    rows = lambda w: pl.BlockSpec((CHUNK, w), lambda i: (i, 0))
    shapes = [(WIDTH, LANES), (LATENT, LANES), (LANES, WIDTH), (LANES, LATENT)]
    return pl.pallas_call(
        lay_out_kernel,
        grid=(STEPS,),
        in_specs=[wide(WIDTH), wide(LATENT)],
        out_specs=[columns(WIDTH), columns(LATENT), rows(WIDTH), rows(LATENT)],
        out_shape=[jax.ShapeDtypeStruct(shape, BF16) for shape in shapes],
        compiler_params=pltpu.CompilerParams(
            dimension_semantics=("arbitrary",), vmem_limit_bytes=60 * 1024 * 1024
        ),
        cost_estimate=pl.CostEstimate(flops=0, bytes_accessed=14 * 10**6, transcendentals=0),
        name="lay_out",
    )(query, grad)


def turn_back_kernel(width, x_ref, out_ref):
    x = x_ref[...]
    out_ref[...] = jnp.concatenate(
        [x[:, h * ROWS:(h + 1) * ROWS] for h in range(HEADS)], axis=0
    ).T


def turn_back(x):
    width = x.shape[0]
    return pl.pallas_call(
        lambda *refs: turn_back_kernel(width, *refs),
        grid=(STEPS,),
        in_specs=[pl.BlockSpec((width, CHUNK), lambda i: (0, i))],
        out_specs=pl.BlockSpec((ROWS, HEADS * width), lambda i: (0, i)),
        out_shape=jax.ShapeDtypeStruct((ROWS, GROUPS * width), F32),
        compiler_params=pltpu.CompilerParams(
            dimension_semantics=("arbitrary",), vmem_limit_bytes=60 * 1024 * 1024
        ),
        cost_estimate=pl.CostEstimate(
            flops=0, bytes_accessed=2 * 4 * width * LANES, transcendentals=0
        ),
        name="turn_back",
    )(x)


def attend_kernel(segments, qt, gt, qn, gn, *rest):
    pieces = rest[:8]
    o_ref, dq_ref, keep_ref = rest[8:11]
    send_refs = rest[11:15]
    (c_v, ct_v, s_v, e_v, p_st, ds_st, g_st, top_v, inverse_v, dots_v, st_f, st_b, zero_f, zero_b,
     in_sem, out_sem, zero_sem, dq_sem, bounds) = rest[15:]
    step = pl.program_id(0)
    ctx, head = lax.axis_index("ctx"), lax.axis_index("head")
    z, xh, y, xl, core = ctx >> 3, (ctx >> 2) & 1, ctx & 3, head >> 1, head & 1

    @pl.when(step == 0)
    def _():
        def halve(_, ends):
            found = []
            for value, (low, high) in zip((1, 2), ends):
                mid = (low + high) >> 1
                less = (low < high) & (segments[jnp.minimum(mid, SEQ - 1)] < value)
                found.append((jnp.where(less, mid + 1, low), jnp.where(less, high, mid)))
            return tuple(found)

        ends = (jnp.int32(0), jnp.int32(SEQ))
        ends = lax.fori_loop(0, 13, halve, (ends, ends))
        bounds[0], bounds[1] = ends[0][0], ends[1][0]

    second, third = bounds[0], bounds[1]

    def start_of(position):
        return jnp.where(position >= third, third, jnp.where(position >= second, second, 0))

    first_row = ctx * ROWS
    first = start_of(first_row) // KB
    blocks = (first_row + ROWS + KB - 1) // KB - first
    free_low, free_high = start_of(first_row + ROWS - 1), first_row + 1
    token = first_row + (lax.broadcasted_iota(jnp.int32, (1, CHUNK), 1) & (ROWS - 1))
    start = start_of(token)

    def off(kb):
        return pl.multiple_of((first + kb) * KB, KB)

    def blk(kb):
        return pl.multiple_of(kb * KB, KB)

    def live(block):
        return (block >= first) & (block < first + blocks)

    def fetch(piece, to, half):
        return pltpu.make_async_copy(
            piece,
            ct_v.at[
                pl.ds(pl.multiple_of(half * HALF, 32), HALF),
                pl.ds(pl.multiple_of((to - first * (KB // ROWS)) * ROWS, ROWS), ROWS),
            ],
            in_sem.at[to, half],
        )

    def fetch_all():
        for n in range(64):
            other, piece, slot, x = n // 32, n // 8 % 4, n // 2 % 4, n % 2
            half = 1 - core if other else core
            dy = jnp.where(half == 0, RING[slot], RING[piece])
            dz = jnp.where(half == 0, RING[piece], RING[slot])
            to = ((z + dz) & 3) * 8 + (xh ^ x) * 4 + ((y + dy) & 3)

            @pl.when(live(to >> 2))
            def _():
                fetch(pieces[other * 4 + piece].at[slot, x], to, half).start()

    def by_core(act):
        for c in range(NC):
            @pl.when(core == c)
            def _():
                act(c)

    def hand_out(block, kept, sent, sems, act):
        dz, x = ((block >> 1) - z) & 3, (block & 1) ^ xh

        def copies(c):
            ref = keep_ref.at[dz, :, x] if c == 0 else keep_ref.at[:, dz, x]
            act(pltpu.make_async_copy(kept(c), ref, sems.at[0]))
            for r, send_ref in enumerate(send_refs):
                if c == 1:
                    @pl.when(dz == r)
                    def _():
                        act(pltpu.make_async_copy(sent(0), send_ref.at[:, x], sems.at[1 + r]))
                else:
                    act(pltpu.make_async_copy(sent(1).at[r], send_ref.at[dz, x], sems.at[1 + r]))

        by_core(copies)

    def clear(block, act):
        @pl.when(jnp.logical_not(live(block)))
        def _():
            hand_out(block, lambda c: zero_f, lambda c: zero_b, zero_sem.at[block], act)

    def deliver_block(kb, act):
        slot = lax.rem(kb, 2)
        hand_out(
            first + kb, lambda c: st_f.at[slot, :, :, c], lambda c: st_b.at[slot, :, :, c],
            out_sem.at[slot], act,
        )

    def begin(copy):
        copy.start()

    def end(copy):
        copy.wait()

    def chunk(i):
        return pl.ds(pl.multiple_of(i * CHUNK, CHUNK), CHUNK)

    def score(kb, masked, i):
        s = jnp.dot(
            c_v[pl.ds(blk(kb), KB), :], qt[:, chunk(i)], preferred_element_type=F32
        )
        if masked:
            key = off(kb) + lax.broadcasted_iota(jnp.int32, (KB, CHUNK), 0)
            s = jnp.where((key >= start) & (key <= token), s, NEG)
        return s

    def folded(x):
        return x.reshape(KB // 8, 8, CHUNK)

    def keep_score(kb, s, top):
        s_v[pl.ds(blk(kb), KB), :] = s
        return jnp.maximum(top, jnp.max(folded(s), axis=0))

    lowest = jnp.full((8, CHUNK), NEG, F32)

    @pl.when(step == 0)
    def _():
        fetch_all()
        zero_f[...] = jnp.zeros_like(zero_f)
        zero_b[...] = jnp.zeros_like(zero_b)
        for block in range(SEQ // KB):
            clear(block, begin)

        def turn(kb, top):
            for t in range(KB // ROWS):
                for half in range(2):
                    fetch(pieces[0].at[0, 0], (first + kb) * (KB // ROWS) + t, half).wait()
            c_v[pl.ds(blk(kb), KB), :] = ct_v[:, pl.ds(blk(kb), KB)].T
            return keep_score(kb, score(kb, True, 0), top)

        top_v[...] = lax.fori_loop(0, blocks, turn, lowest)

    top = jnp.max(top_v[...], axis=0, keepdims=True)
    lanes = chunk(step)

    def sweep(body, carried):
        pairs = blocks // 2
        carried = lax.fori_loop(0, pairs, lambda i, c: body(2 * i, 2, c), carried)
        return lax.fori_loop(2 * pairs, blocks, lambda i, c: body(i, 1, c), carried)

    def values(kb, n, ahead, masked, carried):
        total, above = carried
        s = [None] * n
        for i in range(n):
            if ahead:
                s[i] = score(kb + i, masked, step + 1)
            rows = pl.ds(blk(kb + i), KB)
            e = jnp.exp((s_v[rows, :] - top) * SCALE)
            total = total + folded(e).sum(axis=0)
            e_v[rows, lanes] = e.astype(BF16)
        o_ref[...] += jnp.dot(
            ct_v[:LATENT, pl.ds(blk(kb), n * KB)], e_v[pl.ds(blk(kb), n * KB), lanes],
            preferred_element_type=F32,
        )
        if ahead:
            for i in range(n):
                above = keep_score(kb + i, s[i], above)
        return total, above

    def conclude(total):
        inverse = 1.0 / jnp.sum(total, axis=0, keepdims=True)
        out = o_ref[...] * inverse
        o_ref[...] = out
        inverse_v[0:1, lanes] = inverse
        dots_v[0:1, lanes] = jnp.sum(gt[:, lanes].astype(F32) * out, axis=0, keepdims=True)

    o_ref[...] = jnp.zeros_like(o_ref)
    nothing = jnp.zeros((8, CHUNK), F32)

    @pl.when(step < STEPS - 1)
    def _():
        def both(kb, n, carried):
            free = (off(kb) >= free_low) & (off(kb) + n * KB <= free_high)
            return lax.cond(
                free,
                lambda c: values(kb, n, True, False, c),
                lambda c: values(kb, n, True, True, c),
                carried,
            )

        total, top_v[...] = sweep(both, (nothing, lowest))
        conclude(total)

    @pl.when(step == STEPS - 1)
    def _():
        def only(kb, n, carried):
            return values(kb, n, False, None, carried)

        conclude(sweep(only, (nothing, lowest))[0])

        def dq_rows(i):
            return pl.ds(i * WIDTH, WIDTH)

        s_v[:STEPS * WIDTH, :] = jnp.zeros((STEPS * WIDTH, CHUNK), F32)

        def stage(slot):
            turned = g_st[...].T
            for t in range(NY):
                tile = turned[:, t * ROWS:(t + 1) * ROWS].reshape(NXL, NC, PART, ROWS)
                for side in range(NXL):
                    st_f[slot, (t - y) & 3, side ^ xl] = tile[side]
                    st_b[slot, (t - y) & 3, side ^ xl] = tile[side].astype(BF16)

        def weight_grads(kb, i):
            return jnp.dot(
                c_v[pl.ds(blk(kb), KB), :LATENT], gt[:, i * CHUNK:(i + 1) * CHUNK],
                preferred_element_type=F32,
            )

        def back(kb, _):
            @pl.when(kb >= 3)
            def _():
                deliver_block(kb - 3, end)

            rows = pl.ds(blk(kb), KB)
            w = weight_grads(kb, 0)
            stage(lax.rem(kb + 1, 2))
            for i in range(STEPS):
                cols = slice(i * CHUNK, (i + 1) * CHUNK)
                after = weight_grads(kb, i + 1) if i + 1 < STEPS else None
                p = e_v[rows, cols].astype(F32) * inverse_v[0:1, cols]
                p_st[:, cols] = p.astype(BF16)
                ds = (p * (w - dots_v[0:1, cols]) * SCALE).astype(BF16)
                ds_st[:, cols] = ds
                s_v[dq_rows(i), :] += jnp.dot(ct_v[:, rows], ds, preferred_element_type=F32)
                w = after
            dk = jnp.dot(ds_st[...], qn[...], preferred_element_type=F32)
            dv = jnp.dot(p_st[...], gn[...], preferred_element_type=F32)
            g_st[:, :LATENT] = dk[:, :LATENT] + dv
            g_st[:, LATENT:] = dk[:, LATENT:]

            @pl.when(kb >= 1)
            def _():
                deliver_block(kb - 1, begin)

            return 0

        lax.fori_loop(0, blocks, back, 0)
        sends = [
            pltpu.make_async_copy(
                s_v.at[dq_rows(i)], dq_ref.at[:, pl.ds(i * CHUNK, CHUNK)], dq_sem.at[i]
            )
            for i in range(STEPS)
        ]
        for copy in sends:
            copy.start()

        @pl.when(blocks >= 3)
        def _():
            deliver_block(blocks - 3, end)

        stage(lax.rem(blocks + 1, 2))
        deliver_block(blocks - 1, begin)

        def finish(kb, _):
            deliver_block(kb, end)
            return 0

        lax.fori_loop(jnp.maximum(blocks - 2, 0), blocks, finish, 0)
        for block in range(SEQ // KB):
            clear(block, end)
        for copy in sends:
            copy.wait()


def attend(segments, qt, gt, qn, gn, pieces):
    any_spec = pl.BlockSpec(memory_space=pl.ANY)
    whole = lambda shape: pl.BlockSpec(
        shape, lambda i, s: (0, 0), pipeline_mode=pl.Buffered(1)
    )
    tile = (NY, NXL, PART, ROWS)
    staged = (2, NY, NXL, NC, PART, ROWS)
    rings = (NZ, NY, NXH, NXL, PART, ROWS)
    return pl.pallas_call(
        attend_kernel,
        grid_spec=pltpu.PrefetchScalarGridSpec(
            num_scalar_prefetch=1,
            grid=(STEPS,),
            in_specs=[
                whole((WIDTH, LANES)),
                whole((LATENT, LANES)),
                whole((LANES, WIDTH)),
                whole((LANES, LATENT)),
            ] + [any_spec] * 8,
            out_specs=[
                pl.BlockSpec((LATENT, CHUNK), lambda i, s: (0, i)),
            ] + [any_spec] * 6,
            scratch_shapes=[
                pltpu.VMEM((MAXB * KB, WIDTH), BF16),
                pltpu.VMEM((WIDTH, MAXB * KB), BF16),
                pltpu.VMEM((MAXB * KB, CHUNK), F32),
                pltpu.VMEM((MAXB * KB, LANES), BF16),
                pltpu.VMEM((KB, LANES), BF16),
                pltpu.VMEM((KB, LANES), BF16),
                pltpu.VMEM((KB, WIDTH), F32),
                pltpu.VMEM((8, CHUNK), F32),
                pltpu.VMEM((8, LANES), F32),
                pltpu.VMEM((8, LANES), F32),
                pltpu.VMEM(staged, F32),
                pltpu.VMEM(staged, BF16),
                pltpu.VMEM(tile, F32),
                pltpu.VMEM(tile, BF16),
                pltpu.SemaphoreType.DMA((SEQ // ROWS, 2)),
                pltpu.SemaphoreType.DMA((2, 5)),
                pltpu.SemaphoreType.DMA((SEQ // KB, 5)),
                pltpu.SemaphoreType.DMA((STEPS,)),
                pltpu.SMEM((2,), jnp.int32),
            ],
        ),
        out_shape=[
            jax.ShapeDtypeStruct((LATENT, LANES), F32),
            jax.ShapeDtypeStruct((WIDTH, LANES), F32),
            jax.ShapeDtypeStruct(rings, F32),
        ] + [jax.ShapeDtypeStruct(rings[1:], BF16)] * 4,
        compiler_params=pltpu.CompilerParams(
            dimension_semantics=("arbitrary",), vmem_limit_bytes=60 * 1024 * 1024
        ),
        cost_estimate=pl.CostEstimate(
            flops=40 * 10**9, bytes_accessed=30 * 10**6, transcendentals=10**7
        ),
        name="attend",
    )(segments, qt, gt, qn, gn, *pieces)


def deliver(keep, out, attended, query_grad):
    def part(i):
        return keep[i] + send(out[i], other_core).astype(F32)

    def wide(x):
        return x.astype(F32)

    far, attended = lax.optimization_barrier((part(2).astype(BF16), attended))
    far = send(far, along(0, 1))
    attended = turn_back(attended)
    below = part(3).astype(BF16)
    up = (part(1) + wide(far)).astype(BF16)
    up, attended, query_grad = lax.optimization_barrier((up, attended, query_grad))
    up, down = send(up, along(0, 1)), send(below, along(0, 3))
    query_grad = turn_back(query_grad)
    total = part(0) + wide(up) + wide(down)
    parts, query_grad = lax.optimization_barrier((total.astype(BF16), query_grad))
    ring = [wide(send(parts[d], along(1, d))) for d in (1, 3, 2)]
    total = total[0] + ring[0] + ring[1] + ring[2]
    parts = total.astype(BF16)
    ring = [wide(send(parts[a, b], along_x(a, b))) for a, b in ((0, 1), (1, 1), (1, 0))]
    return attended, query_grad, (total[0, 0] + ring[0] + ring[1] + ring[2]).T


def shards(query, compressed, segments, grad_attn):
    pieces, rows = collect(compressed, lax.axis_index("head") % NC, query, grad_attn)
    attended, query_grad, keep, *out = attend(segments, *rows, pieces)
    return deliver(keep, out, attended, query_grad)


def solution(mesh):
    placed = (P("ctx", "head"), P("ctx", None), P(), P("ctx", "head"))
    return jax.shard_map(
        shards,
        mesh=mesh,
        in_specs=placed,
        out_specs=(P("ctx", "head"), P("ctx", "head"), P("ctx", "head")),
        check_vma=False,
    )
```

```python
import math

import jax
import jax.numpy as jnp
from jax import lax
from jax.experimental import pallas as pl
from jax.experimental.pallas import tpu as pltpu
from jax.sharding import PartitionSpec as P

LATENT = 512
ROPE = 64
WIDTH = LATENT + ROPE
ROWS = 128
GROUPS = 16
LANES = ROWS * GROUPS
SEQ = 4096
HALF = WIDTH // 2
PART = WIDTH // 4
KB = 512
MAXB = 7
HEADS = 4
CHUNK = HEADS * ROWS
STEPS = LANES // CHUNK

SCALE = 1.0 / math.sqrt(192.0)
NEG = -1e30

NZ, NXH, NY, NXL, NC = 4, 2, 4, 2, 2
F32, BF16 = jnp.float32, jnp.bfloat16


def flat(z, xh, y, xl, c):
    return ((z * NXH + xh) * NY + y) * (NXL * NC) + xl * NC + c


def send(x, move):
    pairs = []
    for z in range(NZ):
        for xh in range(NXH):
            for y in range(NY):
                for xl in range(NXL):
                    for c in range(NC):
                        to = move(z, xh, y, xl, c)
                        pairs.append((flat(z, xh, y, xl, c), flat(*to)))
    return lax.ppermute(x, ("ctx", "head"), pairs)


def other_core(z, xh, y, xl, c):
    return (z, xh, y, xl, 1 - c)


def across_x(z, xh, y, xl, c):
    return (z, 1 - xh, y, 1 - xl, c)


def along_x(dxh, dxl):
    return lambda z, xh, y, xl, c: (z, (xh + dxh) % NXH, y, (xl + dxl) % NXL, c)


def along(axis, d):
    def move(z, xh, y, xl, c):
        if c == axis:
            return ((z + d) % NZ, xh, y, xl, c)
        return (z, xh, (y + d) % NY, xl, c)

    return move


def collect(own, core, query, grad):
    mine = lax.dynamic_slice_in_dim(own.T, core * HALF, HALF, 0)
    pair = jnp.stack([mine, send(mine, across_x)])
    near = jnp.stack([pair] + [send(pair, along(1, d)) for d in (1, 3, 2)])
    near, query, grad = lax.optimization_barrier((near, query, grad))
    below, above = send(near, along(0, 1)), send(near, along(0, 3))
    below, rows = lax.optimization_barrier((below, lay_out(query, grad)))
    pieces = [near, below, above, send(below, along(0, 1))]
    return pieces + [send(p, other_core) for p in pieces], rows


RING = (0, -1, 1, 2)


def lay_out_kernel(q_ref, g_ref, qt_ref, gt_ref, qn_ref, gn_ref):
    for x_ref, t_ref, n_ref, width in ((q_ref, qt_ref, qn_ref, WIDTH), (g_ref, gt_ref, gn_ref, LATENT)):
        x = x_ref[...]
        turned = x.T
        for h in range(HEADS):
            rows = slice(h * ROWS, (h + 1) * ROWS)
            t_ref[:, rows] = turned[h * width:(h + 1) * width]
            n_ref[rows, :] = x[:, h * width:(h + 1) * width]


def lay_out(query, grad):
    wide = lambda w: pl.BlockSpec((ROWS, HEADS * w), lambda i: (0, i))
    columns = lambda w: pl.BlockSpec((w, CHUNK), lambda i: (0, i))
    rows = lambda w: pl.BlockSpec((CHUNK, w), lambda i: (i, 0))
    shapes = [(WIDTH, LANES), (LATENT, LANES), (LANES, WIDTH), (LANES, LATENT)]
    return pl.pallas_call(
        lay_out_kernel,
        grid=(STEPS,),
        in_specs=[wide(WIDTH), wide(LATENT)],
        out_specs=[columns(WIDTH), columns(LATENT), rows(WIDTH), rows(LATENT)],
        out_shape=[jax.ShapeDtypeStruct(shape, BF16) for shape in shapes],
        compiler_params=pltpu.CompilerParams(
            dimension_semantics=("arbitrary",), vmem_limit_bytes=60 * 1024 * 1024
        ),
        cost_estimate=pl.CostEstimate(flops=0, bytes_accessed=14 * 10**6, transcendentals=0),
        name="lay_out",
    )(query, grad)


def turn_back_kernel(width, x_ref, out_ref):
    x = x_ref[...]
    out_ref[...] = jnp.concatenate(
        [x[:, h * ROWS:(h + 1) * ROWS] for h in range(HEADS)], axis=0
    ).T


def turn_back(x):
    width = x.shape[0]
    return pl.pallas_call(
        lambda *refs: turn_back_kernel(width, *refs),
        grid=(STEPS,),
        in_specs=[pl.BlockSpec((width, CHUNK), lambda i: (0, i))],
        out_specs=pl.BlockSpec((ROWS, HEADS * width), lambda i: (0, i)),
        out_shape=jax.ShapeDtypeStruct((ROWS, GROUPS * width), F32),
        compiler_params=pltpu.CompilerParams(
            dimension_semantics=("arbitrary",), vmem_limit_bytes=60 * 1024 * 1024
        ),
        cost_estimate=pl.CostEstimate(
            flops=0, bytes_accessed=2 * 4 * width * LANES, transcendentals=0
        ),
        name="turn_back",
    )(x)


def attend_kernel(segments, qt0, qt, gt, qn, gn, *rest):
    pieces = rest[:8]
    o_ref, dq_ref, keep_ref = rest[8:11]
    send_refs = rest[11:15]
    (c_v, ct_v, s_v, w_v, acc, top_v, st_f, st_b, zero_f, zero_b, in_sem, out_sem,
     zero_sem, bounds) = rest[15:]
    step = pl.program_id(0)
    ctx, head = lax.axis_index("ctx"), lax.axis_index("head")
    z, xh, y, xl, core = ctx >> 3, (ctx >> 2) & 1, ctx & 3, head >> 1, head & 1

    @pl.when(step == 0)
    def _():
        def halve(_, ends):
            found = []
            for value, (low, high) in zip((1, 2), ends):
                mid = (low + high) >> 1
                less = (low < high) & (segments[jnp.minimum(mid, SEQ - 1)] < value)
                found.append((jnp.where(less, mid + 1, low), jnp.where(less, high, mid)))
            return tuple(found)

        ends = (jnp.int32(0), jnp.int32(SEQ))
        ends = lax.fori_loop(0, 13, halve, (ends, ends))
        bounds[0], bounds[1] = ends[0][0], ends[1][0]

    second, third = bounds[0], bounds[1]

    def start_of(position):
        return jnp.where(position >= third, third, jnp.where(position >= second, second, 0))

    first_row = ctx * ROWS
    first = start_of(first_row) // KB
    blocks = (first_row + ROWS + KB - 1) // KB - first
    free_low, free_high = start_of(first_row + ROWS - 1), first_row + 1
    token = first_row + (lax.broadcasted_iota(jnp.int32, (1, CHUNK), 1) & (ROWS - 1))
    start = start_of(token)

    def off(kb):
        return pl.multiple_of((first + kb) * KB, KB)

    def blk(kb):
        return pl.multiple_of(kb * KB, KB)

    def live(block):
        return (block >= first) & (block < first + blocks)

    def fetch(piece, to, half):
        return pltpu.make_async_copy(
            piece,
            ct_v.at[
                pl.ds(pl.multiple_of(half * HALF, 32), HALF),
                pl.ds(pl.multiple_of((to - first * (KB // ROWS)) * ROWS, ROWS), ROWS),
            ],
            in_sem.at[to, half],
        )

    def fetch_all():
        for n in range(64):
            other, piece, slot, x = n // 32, n // 8 % 4, n // 2 % 4, n % 2
            half = 1 - core if other else core
            dy = jnp.where(half == 0, RING[slot], RING[piece])
            dz = jnp.where(half == 0, RING[piece], RING[slot])
            to = ((z + dz) & 3) * 8 + (xh ^ x) * 4 + ((y + dy) & 3)

            @pl.when(live(to >> 2))
            def _():
                fetch(pieces[other * 4 + piece].at[slot, x], to, half).start()

    def by_core(act):
        for c in range(NC):
            @pl.when(core == c)
            def _():
                act(c)

    def hand_out(block, kept, sent, sems, act):
        dz, x = ((block >> 1) - z) & 3, (block & 1) ^ xh

        def copies(c):
            ref = keep_ref.at[dz, :, x] if c == 0 else keep_ref.at[:, dz, x]
            act(pltpu.make_async_copy(kept(c), ref, sems.at[0]))
            for r, send_ref in enumerate(send_refs):
                if c == 1:
                    @pl.when(dz == r)
                    def _():
                        act(pltpu.make_async_copy(sent(0), send_ref.at[:, x], sems.at[1 + r]))
                else:
                    act(pltpu.make_async_copy(sent(1).at[r], send_ref.at[dz, x], sems.at[1 + r]))

        by_core(copies)

    def clear(block, act):
        @pl.when(jnp.logical_not(live(block)))
        def _():
            hand_out(block, lambda c: zero_f, lambda c: zero_b, zero_sem.at[block], act)

    def deliver_block(kb, act):
        slot = lax.rem(kb, 2)
        hand_out(
            first + kb, lambda c: st_f.at[slot, :, :, c], lambda c: st_b.at[slot, :, :, c],
            out_sem.at[slot], act,
        )

    def begin(copy):
        copy.start()

    def end(copy):
        copy.wait()

    def score(kb, n, masked, q):
        rows = n * KB
        s = jnp.dot(c_v[pl.ds(blk(kb), rows), :], q[...], preferred_element_type=F32)
        if masked:
            key = off(kb) + lax.broadcasted_iota(jnp.int32, (rows, CHUNK), 0)
            s = jnp.where((key >= start) & (key <= token), s, NEG)
        return s

    def folded(x):
        return x.reshape(x.shape[0] // 8, 8, CHUNK)

    def keep_score(kb, n, s, top):
        s_v[pl.ds(blk(kb), n * KB), :] = s
        return jnp.maximum(top, jnp.max(folded(s), axis=0))

    lowest = jnp.full((8, CHUNK), NEG, F32)

    @pl.when(step == 0)
    def _():
        fetch_all()
        zero_f[...] = jnp.zeros_like(zero_f)
        zero_b[...] = jnp.zeros_like(zero_b)
        for block in range(SEQ // KB):
            clear(block, begin)

        def turn(kb, top):
            for t in range(KB // ROWS):
                for half in range(2):
                    fetch(pieces[0].at[0, 0], (first + kb) * (KB // ROWS) + t, half).wait()
            c_v[pl.ds(blk(kb), KB), :] = ct_v[:, pl.ds(blk(kb), KB)].T
            acc[pl.ds(blk(kb), KB), :] = jnp.zeros((KB, WIDTH), F32)
            return keep_score(kb, 1, score(kb, 1, True, qt0), top)

        top_v[...] = lax.fori_loop(0, blocks, turn, lowest)

    top = jnp.max(top_v[...], axis=0, keepdims=True)

    def sweep(body, carried):
        pairs = blocks // 2
        carried = lax.fori_loop(0, pairs, lambda i, c: body(2 * i, 2, c), carried)
        return lax.fori_loop(2 * pairs, blocks, lambda i, c: body(i, 1, c), carried)

    def values(kb, n, total):
        rows = pl.ds(blk(kb), n * KB)
        w_v[rows, :] = jnp.dot(c_v[rows, :LATENT], gt[...], preferred_element_type=F32)
        e = jnp.exp((s_v[rows, :] - top) * SCALE)
        s_v[rows, :] = e
        o_ref[...] += jnp.dot(ct_v[:LATENT, rows], e.astype(BF16), preferred_element_type=F32)
        return total + folded(e).sum(axis=0)

    o_ref[...] = jnp.zeros_like(o_ref)
    total = sweep(values, jnp.zeros((8, CHUNK), F32))
    inverse = 1.0 / jnp.sum(total, axis=0, keepdims=True)
    out = o_ref[...] * inverse
    o_ref[...] = out
    dots = jnp.sum(gt[...].astype(F32) * out, axis=0, keepdims=True)

    dq_ref[...] = jnp.zeros_like(dq_ref)

    def grads(kb, n):
        rows = pl.ds(blk(kb), n * KB)
        p = s_v[rows, :] * inverse
        ds = (p * (w_v[rows, :] - dots) * SCALE).astype(BF16)
        dq_ref[...] += jnp.dot(ct_v[:, rows], ds, preferred_element_type=F32)
        dk = jnp.dot(ds, qn[...], preferred_element_type=F32)
        dv = jnp.dot(p.astype(BF16), gn[...], preferred_element_type=F32)
        acc[rows, :LATENT] += dk[:, :LATENT] + dv
        acc[rows, LATENT:] += dk[:, LATENT:]

    @pl.when(step < STEPS - 1)
    def _():
        def both(kb, n, above):
            def body(masked):
                def run(above):
                    s = score(kb, n, masked, qt)
                    grads(kb, n)
                    return keep_score(kb, n, s, above)

                return run

            free = (off(kb) >= free_low) & (off(kb) + n * KB <= free_high)
            return lax.cond(free, body(False), body(True), above)

        top_v[...] = sweep(both, lowest)

    @pl.when(step == STEPS - 1)
    def _():
        grads(0, 1)

        def stage(kb):
            turned = acc[pl.ds(blk(kb), KB), :].T
            slot = lax.rem(kb, 2)
            for t in range(NY):
                tile = turned[:, t * ROWS:(t + 1) * ROWS].reshape(NXL, NC, PART, ROWS)
                for side in range(NXL):
                    st_f[slot, (t - y) & 3, side ^ xl] = tile[side]
                    st_b[slot, (t - y) & 3, side ^ xl] = tile[side].astype(BF16)

        def room(kb):
            @pl.when(kb >= 2)
            def _():
                deliver_block(kb - 2, end)

        def more(kb, _):
            room(kb - 1)
            stage(kb - 1)
            grads(kb, 1)
            deliver_block(kb - 1, begin)
            return 0

        lax.fori_loop(1, blocks, more, 0)
        room(blocks - 1)
        stage(blocks - 1)
        deliver_block(blocks - 1, begin)

        def finish(kb, _):
            deliver_block(kb, end)
            return 0

        lax.fori_loop(jnp.maximum(blocks - 2, 0), blocks, finish, 0)
        for block in range(SEQ // KB):
            clear(block, end)


def attend(segments, qt, gt, qn, gn, pieces):
    any_spec = pl.BlockSpec(memory_space=pl.ANY)
    tile = (NY, NXL, PART, ROWS)
    staged = (2, NY, NXL, NC, PART, ROWS)
    rings = (NZ, NY, NXH, NXL, PART, ROWS)
    return pl.pallas_call(
        attend_kernel,
        grid_spec=pltpu.PrefetchScalarGridSpec(
            num_scalar_prefetch=1,
            grid=(STEPS,),
            in_specs=[
                pl.BlockSpec((WIDTH, CHUNK), lambda i, s: (0, 0)),
                pl.BlockSpec((WIDTH, CHUNK), lambda i, s: (0, jnp.minimum(i + 1, STEPS - 1))),
                pl.BlockSpec((LATENT, CHUNK), lambda i, s: (0, i)),
                pl.BlockSpec((CHUNK, WIDTH), lambda i, s: (i, 0)),
                pl.BlockSpec((CHUNK, LATENT), lambda i, s: (i, 0)),
            ] + [any_spec] * 8,
            out_specs=[
                pl.BlockSpec((LATENT, CHUNK), lambda i, s: (0, i)),
                pl.BlockSpec((WIDTH, CHUNK), lambda i, s: (0, i)),
            ] + [any_spec] * 5,
            scratch_shapes=[
                pltpu.VMEM((MAXB * KB, WIDTH), BF16),
                pltpu.VMEM((WIDTH, MAXB * KB), BF16),
                pltpu.VMEM((MAXB * KB, CHUNK), F32),
                pltpu.VMEM((MAXB * KB, CHUNK), F32),
                pltpu.VMEM((MAXB * KB, WIDTH), F32),
                pltpu.VMEM((8, CHUNK), F32),
                pltpu.VMEM(staged, F32),
                pltpu.VMEM(staged, BF16),
                pltpu.VMEM(tile, F32),
                pltpu.VMEM(tile, BF16),
                pltpu.SemaphoreType.DMA((SEQ // ROWS, 2)),
                pltpu.SemaphoreType.DMA((2, 5)),
                pltpu.SemaphoreType.DMA((SEQ // KB, 5)),
                pltpu.SMEM((2,), jnp.int32),
            ],
        ),
        out_shape=[
            jax.ShapeDtypeStruct((LATENT, LANES), F32),
            jax.ShapeDtypeStruct((WIDTH, LANES), F32),
            jax.ShapeDtypeStruct(rings, F32),
        ] + [jax.ShapeDtypeStruct(rings[1:], BF16)] * 4,
        compiler_params=pltpu.CompilerParams(
            dimension_semantics=("arbitrary",), vmem_limit_bytes=60 * 1024 * 1024
        ),
        cost_estimate=pl.CostEstimate(
            flops=40 * 10**9, bytes_accessed=30 * 10**6, transcendentals=10**7
        ),
        name="attend",
    )(segments, qt, qt, gt, qn, gn, *pieces)


def deliver(keep, out, attended, query_grad):
    def part(i):
        return keep[i] + send(out[i], other_core).astype(F32)

    def wide(x):
        return x.astype(F32)

    far, attended = lax.optimization_barrier((part(2).astype(BF16), attended))
    far = send(far, along(0, 1))
    attended = turn_back(attended)
    below = part(3).astype(BF16)
    up = (part(1) + wide(far)).astype(BF16)
    up, attended, query_grad = lax.optimization_barrier((up, attended, query_grad))
    up, down = send(up, along(0, 1)), send(below, along(0, 3))
    query_grad = turn_back(query_grad)
    total = part(0) + wide(up) + wide(down)
    parts, query_grad = lax.optimization_barrier((total.astype(BF16), query_grad))
    ring = [wide(send(parts[d], along(1, d))) for d in (1, 3, 2)]
    total = total[0] + ring[0] + ring[1] + ring[2]
    parts = total.astype(BF16)
    ring = [wide(send(parts[a, b], along_x(a, b))) for a, b in ((0, 1), (1, 1), (1, 0))]
    return attended, query_grad, (total[0, 0] + ring[0] + ring[1] + ring[2]).T


def shards(query, compressed, segments, grad_attn):
    pieces, rows = collect(compressed, lax.axis_index("head") % NC, query, grad_attn)
    attended, query_grad, keep, *out = attend(segments, *rows, pieces)
    return deliver(keep, out, attended, query_grad)


def solution(mesh):
    placed = (P("ctx", "head"), P("ctx", None), P(), P("ctx", "head"))
    return jax.shard_map(
        shards,
        mesh=mesh,
        in_specs=placed,
        out_specs=(P("ctx", "head"), P("ctx", "head"), P("ctx", "head")),
        check_vma=False,
    )
```

```python
import math

import jax
import jax.numpy as jnp
from jax import lax
from jax.experimental import pallas as pl
from jax.experimental.pallas import tpu as pltpu
from jax.sharding import PartitionSpec as P

LATENT = 512
ROPE = 64
WIDTH = LATENT + ROPE
ROWS = 128
GROUPS = 16
LANES = ROWS * GROUPS
SEQ = 4096
HALF = WIDTH // 2
PART = WIDTH // 4
KB = 512
MAXB = 7
HEADS = 4
CHUNK = HEADS * ROWS
STEPS = LANES // CHUNK

SCALE = 1.0 / math.sqrt(192.0)
NEG = -1e30

NZ, NXH, NY, NXL, NC = 4, 2, 4, 2, 2
F32, BF16 = jnp.float32, jnp.bfloat16


def flat(z, xh, y, xl, c):
    return ((z * NXH + xh) * NY + y) * (NXL * NC) + xl * NC + c


def send(x, move):
    pairs = []
    for z in range(NZ):
        for xh in range(NXH):
            for y in range(NY):
                for xl in range(NXL):
                    for c in range(NC):
                        to = move(z, xh, y, xl, c)
                        pairs.append((flat(z, xh, y, xl, c), flat(*to)))
    return lax.ppermute(x, ("ctx", "head"), pairs)


def other_core(z, xh, y, xl, c):
    return (z, xh, y, xl, 1 - c)


def across_x(z, xh, y, xl, c):
    return (z, 1 - xh, y, 1 - xl, c)


def along_x(dxh, dxl):
    return lambda z, xh, y, xl, c: (z, (xh + dxh) % NXH, y, (xl + dxl) % NXL, c)


def along(axis, d):
    def move(z, xh, y, xl, c):
        if c == axis:
            return ((z + d) % NZ, xh, y, xl, c)
        return (z, xh, (y + d) % NY, xl, c)

    return move


def collect(own, core, query, grad):
    mine = lax.dynamic_slice_in_dim(own.T, core * HALF, HALF, 0)
    pair = jnp.stack([mine, send(mine, across_x)])
    near = jnp.stack([pair] + [send(pair, along(1, d)) for d in (1, 3, 2)])
    near, query, grad = lax.optimization_barrier((near, query, grad))
    below, above = send(near, along(0, 1)), send(near, along(0, 3))
    below, rows = lax.optimization_barrier((below, lay_out(query, grad)))
    pieces = [near, below, above, send(below, along(0, 1))]
    return pieces + [send(p, other_core) for p in pieces], rows


RING = (0, -1, 1, 2)


def lay_out_kernel(q_ref, g_ref, qt_ref, gt_ref, qn_ref, gn_ref):
    for x_ref, t_ref, n_ref, width in ((q_ref, qt_ref, qn_ref, WIDTH), (g_ref, gt_ref, gn_ref, LATENT)):
        x = x_ref[...]
        turned = x.T
        for h in range(HEADS):
            rows = slice(h * ROWS, (h + 1) * ROWS)
            t_ref[:, rows] = turned[h * width:(h + 1) * width]
            n_ref[rows, :] = x[:, h * width:(h + 1) * width]


def lay_out(query, grad):
    wide = lambda w: pl.BlockSpec((ROWS, HEADS * w), lambda i: (0, i))
    columns = lambda w: pl.BlockSpec((w, CHUNK), lambda i: (0, i))
    rows = lambda w: pl.BlockSpec((CHUNK, w), lambda i: (i, 0))
    shapes = [(WIDTH, LANES), (LATENT, LANES), (LANES, WIDTH), (LANES, LATENT)]
    return pl.pallas_call(
        lay_out_kernel,
        grid=(STEPS,),
        in_specs=[wide(WIDTH), wide(LATENT)],
        out_specs=[columns(WIDTH), columns(LATENT), rows(WIDTH), rows(LATENT)],
        out_shape=[jax.ShapeDtypeStruct(shape, BF16) for shape in shapes],
        compiler_params=pltpu.CompilerParams(
            dimension_semantics=("arbitrary",), vmem_limit_bytes=60 * 1024 * 1024
        ),
        cost_estimate=pl.CostEstimate(flops=0, bytes_accessed=14 * 10**6, transcendentals=0),
        name="lay_out",
    )(query, grad)


def turn_back_kernel(width, x_ref, out_ref):
    x = x_ref[...]
    out_ref[...] = jnp.concatenate(
        [x[:, h * ROWS:(h + 1) * ROWS] for h in range(HEADS)], axis=0
    ).T


def turn_back(x):
    width = x.shape[0]
    return pl.pallas_call(
        lambda *refs: turn_back_kernel(width, *refs),
        grid=(STEPS,),
        in_specs=[pl.BlockSpec((width, CHUNK), lambda i: (0, i))],
        out_specs=pl.BlockSpec((ROWS, HEADS * width), lambda i: (0, i)),
        out_shape=jax.ShapeDtypeStruct((ROWS, GROUPS * width), F32),
        compiler_params=pltpu.CompilerParams(
            dimension_semantics=("arbitrary",), vmem_limit_bytes=60 * 1024 * 1024
        ),
        cost_estimate=pl.CostEstimate(
            flops=0, bytes_accessed=2 * 4 * width * LANES, transcendentals=0
        ),
        name="turn_back",
    )(x)


def attend_kernel(segments, qt0, qt, gt, qn, gn, *rest):
    pieces = rest[:8]
    o_ref, dq_ref, keep_ref = rest[8:11]
    send_refs = rest[11:15]
    (c_v, ct_v, s_v, w_v, acc, top_v, st_f, st_b, zero_f, zero_b, in_sem, out_sem,
     zero_sem, bounds) = rest[15:]
    step = pl.program_id(0)
    ctx, head = lax.axis_index("ctx"), lax.axis_index("head")
    z, xh, y, xl, core = ctx >> 3, (ctx >> 2) & 1, ctx & 3, head >> 1, head & 1

    @pl.when(step == 0)
    def _():
        def halve(_, ends):
            found = []
            for value, (low, high) in zip((1, 2), ends):
                mid = (low + high) >> 1
                less = (low < high) & (segments[jnp.minimum(mid, SEQ - 1)] < value)
                found.append((jnp.where(less, mid + 1, low), jnp.where(less, high, mid)))
            return tuple(found)

        ends = (jnp.int32(0), jnp.int32(SEQ))
        ends = lax.fori_loop(0, 13, halve, (ends, ends))
        bounds[0], bounds[1] = ends[0][0], ends[1][0]

    second, third = bounds[0], bounds[1]

    def start_of(position):
        return jnp.where(position >= third, third, jnp.where(position >= second, second, 0))

    first_row = ctx * ROWS
    first = start_of(first_row) // KB
    blocks = (first_row + ROWS + KB - 1) // KB - first
    free_low, free_high = start_of(first_row + ROWS - 1), first_row + 1
    token = first_row + (lax.broadcasted_iota(jnp.int32, (1, CHUNK), 1) & (ROWS - 1))
    start = start_of(token)

    def off(kb):
        return pl.multiple_of((first + kb) * KB, KB)

    def blk(kb):
        return pl.multiple_of(kb * KB, KB)

    def live(block):
        return (block >= first) & (block < first + blocks)

    def fetch(piece, to, half):
        return pltpu.make_async_copy(
            piece,
            ct_v.at[
                pl.ds(pl.multiple_of(half * HALF, 32), HALF),
                pl.ds(pl.multiple_of((to - first * (KB // ROWS)) * ROWS, ROWS), ROWS),
            ],
            in_sem.at[to, half],
        )

    def fetch_all():
        for n in range(64):
            other, piece, slot, x = n // 32, n // 8 % 4, n // 2 % 4, n % 2
            half = 1 - core if other else core
            dy = jnp.where(half == 0, RING[slot], RING[piece])
            dz = jnp.where(half == 0, RING[piece], RING[slot])
            to = ((z + dz) & 3) * 8 + (xh ^ x) * 4 + ((y + dy) & 3)

            @pl.when(live(to >> 2))
            def _():
                fetch(pieces[other * 4 + piece].at[slot, x], to, half).start()

    def by_core(act):
        for c in range(NC):
            @pl.when(core == c)
            def _():
                act(c)

    def hand_out(block, kept, sent, sems, act):
        dz, x = ((block >> 1) - z) & 3, (block & 1) ^ xh

        def copies(c):
            ref = keep_ref.at[dz, :, x] if c == 0 else keep_ref.at[:, dz, x]
            act(pltpu.make_async_copy(kept(c), ref, sems.at[0]))
            for r, send_ref in enumerate(send_refs):
                if c == 1:
                    @pl.when(dz == r)
                    def _():
                        act(pltpu.make_async_copy(sent(0), send_ref.at[:, x], sems.at[1 + r]))
                else:
                    act(pltpu.make_async_copy(sent(1).at[r], send_ref.at[dz, x], sems.at[1 + r]))

        by_core(copies)

    def clear(block, act):
        @pl.when(jnp.logical_not(live(block)))
        def _():
            hand_out(block, lambda c: zero_f, lambda c: zero_b, zero_sem.at[block], act)

    def deliver_block(kb, act):
        slot = lax.rem(kb, 2)
        hand_out(
            first + kb, lambda c: st_f.at[slot, :, :, c], lambda c: st_b.at[slot, :, :, c],
            out_sem.at[slot], act,
        )

    def begin(copy):
        copy.start()

    def end(copy):
        copy.wait()

    def score(kb, n, masked, q):
        rows = n * KB
        s = jnp.dot(c_v[pl.ds(blk(kb), rows), :], q[...], preferred_element_type=F32)
        if masked:
            key = off(kb) + lax.broadcasted_iota(jnp.int32, (rows, CHUNK), 0)
            s = jnp.where((key >= start) & (key <= token), s, NEG)
        return s

    def folded(x):
        return x.reshape(x.shape[0] // 8, 8, CHUNK)

    def keep_score(kb, n, s, top):
        s_v[pl.ds(blk(kb), n * KB), :] = s
        return jnp.maximum(top, jnp.max(folded(s), axis=0))

    lowest = jnp.full((8, CHUNK), NEG, F32)

    @pl.when(step == 0)
    def _():
        fetch_all()
        zero_f[...] = jnp.zeros_like(zero_f)
        zero_b[...] = jnp.zeros_like(zero_b)
        for block in range(SEQ // KB):
            clear(block, begin)

        def turn(kb, top):
            for t in range(KB // ROWS):
                for half in range(2):
                    fetch(pieces[0].at[0, 0], (first + kb) * (KB // ROWS) + t, half).wait()
            c_v[pl.ds(blk(kb), KB), :] = ct_v[:, pl.ds(blk(kb), KB)].T
            acc[pl.ds(blk(kb), KB), :] = jnp.zeros((KB, WIDTH), F32)
            return keep_score(kb, 1, score(kb, 1, True, qt0), top)

        top_v[...] = lax.fori_loop(0, blocks, turn, lowest)

    top = jnp.max(top_v[...], axis=0, keepdims=True)

    def sweep(body, carried):
        threes = blocks // 3
        carried = lax.fori_loop(0, threes, lambda i, c: body(3 * i, 3, c), carried)
        left = blocks - 3 * threes
        carried = lax.fori_loop(0, left >> 1, lambda i, c: body(3 * threes, 2, c), carried)
        return lax.fori_loop(0, left & 1, lambda i, c: body(3 * threes, 1, c), carried)

    def values(kb, n, total):
        rows = pl.ds(blk(kb), n * KB)
        w_v[rows, :] = jnp.dot(c_v[rows, :LATENT], gt[...], preferred_element_type=F32)
        e = jnp.exp((s_v[rows, :] - top) * SCALE)
        s_v[rows, :] = e
        o_ref[...] += jnp.dot(ct_v[:LATENT, rows], e.astype(BF16), preferred_element_type=F32)
        return total + folded(e).sum(axis=0)

    o_ref[...] = jnp.zeros_like(o_ref)
    total = sweep(values, jnp.zeros((8, CHUNK), F32))
    inverse = 1.0 / jnp.sum(total, axis=0, keepdims=True)
    out = o_ref[...] * inverse
    o_ref[...] = out
    dots = jnp.sum(gt[...].astype(F32) * out, axis=0, keepdims=True)

    dq_ref[...] = jnp.zeros_like(dq_ref)

    def grads(kb, n):
        rows = pl.ds(blk(kb), n * KB)
        p = s_v[rows, :] * inverse
        ds = (p * (w_v[rows, :] - dots) * SCALE).astype(BF16)
        dq_ref[...] += jnp.dot(ct_v[:, rows], ds, preferred_element_type=F32)
        dk = jnp.dot(ds, qn[...], preferred_element_type=F32)
        dv = jnp.dot(p.astype(BF16), gn[...], preferred_element_type=F32)
        acc[rows, :LATENT] += dk[:, :LATENT] + dv
        acc[rows, LATENT:] += dk[:, LATENT:]

    @pl.when(step < STEPS - 1)
    def _():
        def both(kb, n, above):
            def body(masked):
                def run(above):
                    s = score(kb, n, masked, qt)
                    grads(kb, n)
                    return keep_score(kb, n, s, above)

                return run

            free = (off(kb) >= free_low) & (off(kb) + n * KB <= free_high)
            return lax.cond(free, body(False), body(True), above)

        top_v[...] = sweep(both, lowest)

    @pl.when(step == STEPS - 1)
    def _():
        grads(0, 1)

        def stage(kb):
            turned = acc[pl.ds(blk(kb), KB), :].T
            slot = lax.rem(kb, 2)
            for t in range(NY):
                tile = turned[:, t * ROWS:(t + 1) * ROWS].reshape(NXL, NC, PART, ROWS)
                for side in range(NXL):
                    st_f[slot, (t - y) & 3, side ^ xl] = tile[side]
                    st_b[slot, (t - y) & 3, side ^ xl] = tile[side].astype(BF16)

        def room(kb):
            @pl.when(kb >= 2)
            def _():
                deliver_block(kb - 2, end)

        def more(kb, _):
            room(kb - 1)
            stage(kb - 1)
            grads(kb, 1)
            deliver_block(kb - 1, begin)
            return 0

        lax.fori_loop(1, blocks, more, 0)
        room(blocks - 1)
        stage(blocks - 1)
        deliver_block(blocks - 1, begin)

        def finish(kb, _):
            deliver_block(kb, end)
            return 0

        lax.fori_loop(jnp.maximum(blocks - 2, 0), blocks, finish, 0)
        for block in range(SEQ // KB):
            clear(block, end)


def attend(segments, qt, gt, qn, gn, pieces):
    any_spec = pl.BlockSpec(memory_space=pl.ANY)
    tile = (NY, NXL, PART, ROWS)
    staged = (2, NY, NXL, NC, PART, ROWS)
    rings = (NZ, NY, NXH, NXL, PART, ROWS)
    return pl.pallas_call(
        attend_kernel,
        grid_spec=pltpu.PrefetchScalarGridSpec(
            num_scalar_prefetch=1,
            grid=(STEPS,),
            in_specs=[
                pl.BlockSpec((WIDTH, CHUNK), lambda i, s: (0, 0)),
                pl.BlockSpec((WIDTH, CHUNK), lambda i, s: (0, jnp.minimum(i + 1, STEPS - 1))),
                pl.BlockSpec((LATENT, CHUNK), lambda i, s: (0, i)),
                pl.BlockSpec((CHUNK, WIDTH), lambda i, s: (i, 0)),
                pl.BlockSpec((CHUNK, LATENT), lambda i, s: (i, 0)),
            ] + [any_spec] * 8,
            out_specs=[
                pl.BlockSpec((LATENT, CHUNK), lambda i, s: (0, i)),
                pl.BlockSpec((WIDTH, CHUNK), lambda i, s: (0, i)),
            ] + [any_spec] * 5,
            scratch_shapes=[
                pltpu.VMEM((MAXB * KB, WIDTH), BF16),
                pltpu.VMEM((WIDTH, MAXB * KB), BF16),
                pltpu.VMEM((MAXB * KB, CHUNK), F32),
                pltpu.VMEM((MAXB * KB, CHUNK), F32),
                pltpu.VMEM((MAXB * KB, WIDTH), F32),
                pltpu.VMEM((8, CHUNK), F32),
                pltpu.VMEM(staged, F32),
                pltpu.VMEM(staged, BF16),
                pltpu.VMEM(tile, F32),
                pltpu.VMEM(tile, BF16),
                pltpu.SemaphoreType.DMA((SEQ // ROWS, 2)),
                pltpu.SemaphoreType.DMA((2, 5)),
                pltpu.SemaphoreType.DMA((SEQ // KB, 5)),
                pltpu.SMEM((2,), jnp.int32),
            ],
        ),
        out_shape=[
            jax.ShapeDtypeStruct((LATENT, LANES), F32),
            jax.ShapeDtypeStruct((WIDTH, LANES), F32),
            jax.ShapeDtypeStruct(rings, F32),
        ] + [jax.ShapeDtypeStruct(rings[1:], BF16)] * 4,
        compiler_params=pltpu.CompilerParams(
            dimension_semantics=("arbitrary",), vmem_limit_bytes=60 * 1024 * 1024
        ),
        cost_estimate=pl.CostEstimate(
            flops=40 * 10**9, bytes_accessed=30 * 10**6, transcendentals=10**7
        ),
        name="attend",
    )(segments, qt, qt, gt, qn, gn, *pieces)


def deliver(keep, out, attended, query_grad):
    def part(i):
        return keep[i] + send(out[i], other_core).astype(F32)

    def wide(x):
        return x.astype(F32)

    far, attended = lax.optimization_barrier((part(2).astype(BF16), attended))
    far = send(far, along(0, 1))
    attended = turn_back(attended)
    below = part(3).astype(BF16)
    up = (part(1) + wide(far)).astype(BF16)
    up, attended, query_grad = lax.optimization_barrier((up, attended, query_grad))
    up, down = send(up, along(0, 1)), send(below, along(0, 3))
    query_grad = turn_back(query_grad)
    total = part(0) + wide(up) + wide(down)
    parts, query_grad = lax.optimization_barrier((total.astype(BF16), query_grad))
    ring = [wide(send(parts[d], along(1, d))) for d in (1, 3, 2)]
    total = total[0] + ring[0] + ring[1] + ring[2]
    parts = total.astype(BF16)
    ring = [wide(send(parts[a, b], along_x(a, b))) for a, b in ((0, 1), (1, 1), (1, 0))]
    return attended, query_grad, (total[0, 0] + ring[0] + ring[1] + ring[2]).T


def shards(query, compressed, segments, grad_attn):
    pieces, rows = collect(compressed, lax.axis_index("head") % NC, query, grad_attn)
    attended, query_grad, keep, *out = attend(segments, *rows, pieces)
    return deliver(keep, out, attended, query_grad)


def solution(mesh):
    placed = (P("ctx", "head"), P("ctx", None), P(), P("ctx", "head"))
    return jax.shard_map(
        shards,
        mesh=mesh,
        in_specs=placed,
        out_specs=(P("ctx", "head"), P("ctx", "head"), P("ctx", "head")),
        check_vma=False,
    )
```
